128 devices in a mesh: seq: 16 (over z, x), inter: 8 (over y, core).
Axes of the slice: x: 4, y: 4, z: 4, core: 2. Of those that a mesh axis runs over, the one named last changes fastest.
Arguments:
- queries: bfloat16 [2, 16, 512, 4096], P(None, 'seq', 'inter'), may hold values from -12 to 12
- span_keys: bfloat16 [2, 16, 512, 1024], P(None, 'seq', None, 'inter'), may hold values from -6 to 6
- span_values: bfloat16 [2, 16, 512, 1024], P(None, 'seq', None, 'inter'), may hold values from -6 to 6
- cache_keys: bfloat16 [32, 16, 512, 1024], P(None, 'seq', None, 'inter'), may hold values from -6 to 6
- cache_values: bfloat16 [32, 16, 512, 1024], P(None, 'seq', None, 'inter'), may hold values from -6 to 6
- block_key_scales: bfloat16 [32, 16, 8], P(None, 'seq', 'inter'), may hold values from 0.5 to 2
- value_scales: bfloat16 [32, 16, 8], P(None, 'seq', 'inter'), may hold values from 0.5 to 2
- selections: int32 [2, 16, 8, 3], P(None, 'seq', 'inter'), may hold values from 0 to 511, as said below
- start: int32 [1], replicated, may hold values from 253952 to 262144
Outputs:
- attended: bfloat16 [2, 16, 512, 4096], P(None, 'seq', 'inter')
The draws below stay inside these ranges and needn't reach their ends.
Inputs may be any that keep to these rules, and one draw needn't show every extreme that they name: `selections`: cache block numbers. The three of one query block and group differ; the first lies in the last 16 blocks of the cache. For one group and one index s of seq, the 6 blocks selected by its query blocks have at most 2 on any one index b % 16, and exactly 2 on some.
All inputs are finite; a program needn't handle non-finite values.
Results may differ from the reference program's by a relative error of at most 0.0038.
Values may be sent and summed in bfloat16 or wider, within the bound.
A program may use at most 128 MiB of HBM per device.

```python
import math
import jax
import jax.numpy as jnp
from jax import lax

H = 32
KEY_GROUPS = 8
DH = 128
BLK = 512
QB_DEV = 2
KVB_DEV = 32
HG = 4
CACHE_BLOCKS = 512
CAP = 2
N_SEQ = 16


def draw_queries(key, part):
    key = jax.random.fold_in(key, 3)
    first_key = jax.random.fold_in(key, 0)
    drawn = jnp.clip(jax.random.normal(first_key, (QB_DEV, N_SEQ, BLK, H * DH), jnp.float32), -6.0, 6.0)
    return drawn.astype(jnp.bfloat16)


def draw_cache_keys(key, part):
    key = jax.random.fold_in(key, 5)
    first_key = jax.random.fold_in(key, 0)
    drawn = jnp.clip(jax.random.normal(first_key, (KVB_DEV, N_SEQ, BLK, KEY_GROUPS * DH), jnp.float32), -6.0, 6.0)
    return drawn.astype(jnp.bfloat16)


def draw_selections(key, part):
    key = jax.random.fold_in(key, 11)
    item_count = 3 * QB_DEV
    slot_count = CAP * N_SEQ

    def single_list(sub_key):
        keys_split = jax.random.split(sub_key, 5)
        labels = jax.random.permutation(keys_split[0], N_SEQ).astype(jnp.int32)
        others = jax.random.permutation(keys_split[1], slot_count - CAP).astype(jnp.int32) + CAP
        places = jnp.concatenate([jnp.arange(CAP, dtype=jnp.int32), others[:item_count - CAP]])
        places = jax.random.permutation(keys_split[2], places)
        owners = labels[places // CAP].reshape(QB_DEV, 3)
        first_row = jax.random.randint(keys_split[3], (QB_DEV,), 0, KVB_DEV - 1)
        second_row = (first_row + 1 + jax.random.randint(keys_split[4], (QB_DEV,), 0, KVB_DEV - 2)) % (KVB_DEV - 1)
        last_row = jnp.full((QB_DEV,), KVB_DEV - 1, jnp.int32)
        rows_used = jnp.stack([last_row, first_row.astype(jnp.int32), second_row.astype(jnp.int32)], axis=-1)
        return rows_used * N_SEQ + owners
    lists = jax.vmap(single_list)(jax.random.split(key, N_SEQ * KEY_GROUPS))
    return jnp.transpose(lists.reshape(N_SEQ, KEY_GROUPS, QB_DEV, 3), (2, 0, 1, 3)).astype(jnp.int32)


def block_levels(rng, shape, cuts, smallest, high):
    gain = 1.0
    for position, shards_of in cuts:
        steps = jax.random.uniform(jax.random.fold_in(jax.random.fold_in(rng, 6), position), (shards_of,), jnp.float32, smallest / len(cuts), high / len(cuts))
        gain = gain * jnp.repeat(jnp.exp(steps), shape[position] // shards_of).reshape((-1,) + (1,) * (len(shape) - 1 - position))
    return gain


def normal_values(key, dims, spread, limit, pieces=(), kind=jnp.bfloat16):
    loudness = block_levels(key, dims, pieces, -0.22, 0.18) if pieces else 1.0
    values = jax.random.normal(key, dims, jnp.float32) * spread * loudness
    return jnp.minimum(jnp.maximum(values, -limit), limit).astype(kind)


def setup_inputs(seed: int = 0) -> dict:
    keys = jax.random.split(jax.random.key(seed), 10)
    queries = draw_queries(jax.random.fold_in(keys[9], 71), 0)
    span_keys = normal_values(keys[1], (QB_DEV, N_SEQ, BLK, KEY_GROUPS * DH), 1.0, 6.0, ((1, 16), (3, 8)))
    span_values = normal_values(keys[2], (QB_DEV, N_SEQ, BLK, KEY_GROUPS * DH), 1.0, 6.0, ((1, 16), (3, 8)))
    cache_keys = draw_cache_keys(jax.random.fold_in(keys[9], 71), 0)
    cache_values = normal_values(keys[4], (KVB_DEV, N_SEQ, BLK, KEY_GROUPS * DH), 1.0, 6.0, ((1, 16), (3, 8)))
    block_key_scales = jnp.clip(jnp.exp(math.log(2.0) - 1.3862944 * jax.random.uniform(keys[5], (KVB_DEV, N_SEQ, KEY_GROUPS), jnp.float32) ** block_levels(keys[5], (KVB_DEV, N_SEQ, KEY_GROUPS), ((1, 16), (2, 8)), -0.2, 0.2)), 0.5, 2.0).astype(jnp.bfloat16)
    value_scales = jnp.clip(jnp.exp(math.log(2.0) - 1.3862944 * jax.random.uniform(keys[6], (KVB_DEV, N_SEQ, KEY_GROUPS), jnp.float32) ** block_levels(keys[6], (KVB_DEV, N_SEQ, KEY_GROUPS), ((1, 16), (2, 8)), -0.2, 0.2)), 0.5, 2.0).astype(jnp.bfloat16)
    selections = draw_selections(jax.random.fold_in(keys[9], 71), 0)
    start = jax.random.randint(keys[8], (1,), (CACHE_BLOCKS - N_SEQ) * BLK, CACHE_BLOCKS * BLK + 1).astype(jnp.int32)
    return dict(queries=queries, span_keys=span_keys, span_values=span_values, cache_keys=cache_keys, cache_values=cache_values, block_key_scales=block_key_scales, value_scales=value_scales, selections=selections, start=start)


def attend(query_vector, own_keys, own_values, chosen_keys, chosen_values, key_scale, value_scale, sel_blocks, cutoff, positions):
    row_count = query_vector.shape[0]
    head_count = query_vector.shape[1]
    head_dim = query_vector.shape[2]
    block_len = own_keys.shape[0]
    all_keys = jnp.concatenate([own_keys, chosen_keys.reshape(-1, head_dim)], axis=0)
    flat_query = query_vector.reshape(row_count * head_count, head_dim)
    scores = lax.dot_general(flat_query, all_keys, (((1,), (1,)), ((), ())), preferred_element_type=jnp.float32)
    column_scale = jnp.concatenate([jnp.ones((block_len,), jnp.float32), jnp.repeat(key_scale.astype(jnp.float32), block_len)])
    scores = scores * (column_scale / math.sqrt(head_dim))
    scores = scores.reshape(row_count, head_count, -1)
    key_index = jnp.arange(block_len, dtype=jnp.int32)
    own_ok = positions[:, None] >= key_index[None, :]
    sel_ok = (sel_blocks[:, None] * block_len + key_index[None, :] < cutoff).reshape(-1)
    allowed = jnp.concatenate([own_ok, jnp.broadcast_to(sel_ok[None, :], (row_count, sel_ok.shape[0]))], axis=1)[:, None, :]
    top_score = lax.optimization_barrier(jnp.max(jnp.where(allowed, scores, -jnp.inf), axis=-1, keepdims=True))
    weights = jnp.where(allowed, jnp.exp(jnp.where(allowed, scores, top_score) - top_score), 0.0)
    total = lax.optimization_barrier(jnp.sum(weights, axis=-1, keepdims=True))
    rounded = weights.astype(jnp.bfloat16).reshape(row_count * head_count, -1)
    summed = jnp.dot(rounded[:, :block_len], own_values, preferred_element_type=jnp.float32)
    for index in range(chosen_values.shape[0]):
        piece = rounded[:, (index + 1) * block_len:(index + 2) * block_len]
        summed = summed + value_scale[index].astype(jnp.float32) * jnp.dot(piece, chosen_values[index], preferred_element_type=jnp.float32)
    return (summed.reshape(row_count, head_count, head_dim) / total).astype(jnp.bfloat16)

def reference(queries, span_keys, span_values, cache_keys, cache_values, block_key_scales, value_scales, selections, start):
    block_count = QB_DEV * N_SEQ
    query_all = queries.reshape(block_count, BLK, KEY_GROUPS, HG, DH)
    own_keys = span_keys.reshape(block_count, BLK, KEY_GROUPS, DH)
    own_values = span_values.reshape(block_count, BLK, KEY_GROUPS, DH)
    lists = selections.reshape(block_count, KEY_GROUPS, 3)
    flat_keys = cache_keys.reshape(CACHE_BLOCKS, BLK, KEY_GROUPS, DH)
    flat_values = cache_values.reshape(CACHE_BLOCKS, BLK, KEY_GROUPS, DH)
    flattened_key_scale = block_key_scales.reshape(CACHE_BLOCKS, KEY_GROUPS)
    flat_vscale = value_scales.reshape(CACHE_BLOCKS, KEY_GROUPS)
    cutoff = start[0]
    positions = jnp.arange(BLK, dtype=jnp.int32)
    group_position_index = jnp.arange(KEY_GROUPS, dtype=jnp.int32)[:, None]

    def attend_item(inputs):
        query_vector, local_keys, local_values, block_table = inputs
        chosen_keys = flat_keys[block_table, :, group_position_index, :]
        chosen_values = flat_values[block_table, :, group_position_index, :]
        key_scale_factor = flattened_key_scale[block_table, group_position_index]
        value_scale_factor = flat_vscale[block_table, group_position_index]

        def group_results(qq, kk, vv, skk, svv, kss, vss, bb):
            return attend(qq, kk, vv, skk, svv, kss, vss, bb, cutoff, positions)
        return jax.vmap(group_results, in_axes=(1, 1, 1, 0, 0, 0, 0, 0), out_axes=1)(query_vector, local_keys, local_values, chosen_keys, chosen_values, key_scale_factor, value_scale_factor, block_table)
    result = lax.map(attend_item, (query_all, own_keys, own_values, lists))
    return result.reshape(QB_DEV, N_SEQ, BLK, H * DH)
```

```python
import functools
import math

import jax
import jax.numpy as jnp
import numpy as np
from jax import lax
from jax.experimental import pallas as pl
from jax.experimental.pallas import tpu as pltpu
from jax.sharding import PartitionSpec as P

DH = 128
BLK = 512
HG = 4
SIDE = 4
NODES = SIDE * SIDE
ROWS_KV = 32
SLOTS = 7
SLOTS_FIRST = 6
CANDS = 8
PEERS = 8
QROWS = BLK // PEERS
WIDE = HG * DH
TILE_ROWS = HG * QROWS
POOL = ROWS_KV + 4 * SLOTS
LOG2E = 1.4426950408889634
NEG = -1e30
MESH = pl.DeviceIdType.MESH


def attend(
    query_vector,
    own_keys,
    own_values,
    chosen_keys,
    chosen_values,
    key_scale,
    value_scale,
    sel_blocks,
    cutoff,
    positions,
):
    row_count = query_vector.shape[0]
    head_count = query_vector.shape[1]
    head_dim = query_vector.shape[2]
    block_len = own_keys.shape[0]
    all_keys = jnp.concatenate([own_keys, chosen_keys.reshape(-1, head_dim)], axis=0)
    flat_query = query_vector.reshape(row_count * head_count, head_dim)
    scores = lax.dot_general(
        flat_query, all_keys, (((1,), (1,)), ((), ())), preferred_element_type=jnp.float32
    )
    column_scale = jnp.concatenate(
        [jnp.ones((block_len,), jnp.float32), jnp.repeat(key_scale.astype(jnp.float32), block_len)]
    )
    scores = scores * (column_scale / math.sqrt(head_dim))
    scores = scores.reshape(row_count, head_count, -1)
    key_index = jnp.arange(block_len, dtype=jnp.int32)
    own_ok = positions[:, None] >= key_index[None, :]
    sel_ok = (sel_blocks[:, None] * block_len + key_index[None, :] < cutoff).reshape(-1)
    allowed = jnp.concatenate(
        [own_ok, jnp.broadcast_to(sel_ok[None, :], (row_count, sel_ok.shape[0]))], axis=1
    )[:, None, :]
    top_score = jnp.max(jnp.where(allowed, scores, -jnp.inf), axis=-1, keepdims=True)
    weights = jnp.where(allowed, jnp.exp(jnp.where(allowed, scores, top_score) - top_score), 0.0)
    total = jnp.sum(weights, axis=-1, keepdims=True)
    rounded = weights.astype(jnp.bfloat16).reshape(row_count * head_count, -1)
    summed = jnp.dot(rounded[:, :block_len], own_values, preferred_element_type=jnp.float32)
    for index in range(chosen_values.shape[0]):
        piece = rounded[:, (index + 1) * block_len : (index + 2) * block_len]
        summed = summed + value_scale[index].astype(jnp.float32) * jnp.dot(
            piece, chosen_values[index], preferred_element_type=jnp.float32
        )
    return (summed.reshape(row_count, head_count, head_dim) / total).astype(jnp.bfloat16)


def exchange_all(
    queries,
    span_keys,
    span_values,
    cache_keys,
    cache_values,
    block_key_scales,
    value_scales,
    selections,
    start,
):
    blocks_here = queries.shape[0]
    groups_here = selections.shape[2]
    stored_blocks = cache_keys.shape[0]
    seq_count = lax.axis_size("seq")
    seq_rank = lax.axis_index("seq")
    item_count = 3 * blocks_here
    capacity = max(2, (item_count + seq_count - 1) // seq_count)
    cutoff = start[0]
    listed = lax.all_gather(selections, "seq", axis=1, tiled=True)
    wanted = jnp.transpose(listed, (1, 2, 0, 3)).reshape(seq_count, groups_here, item_count)
    owner_rank = wanted % seq_count
    local_row = wanted // seq_count
    is_mine = (owner_rank == seq_rank).astype(jnp.int32)
    ranking = jnp.cumsum(is_mine, axis=2) - 1
    slot_ids = jnp.arange(capacity, dtype=jnp.int32)
    slot_hits = (is_mine[..., None] == 1) & (ranking[..., None] == slot_ids)
    slot_block = jnp.sum(jnp.where(slot_hits, local_row[..., None], 0), axis=2)
    group_ids = jnp.arange(groups_here, dtype=jnp.int32)[None, :, None]
    stored_keys = cache_keys[:, 0].reshape(stored_blocks, BLK, groups_here, DH)
    stored_values = cache_values[:, 0].reshape(stored_blocks, BLK, groups_here, DH)
    picked_keys = stored_keys[slot_block, :, group_ids, :]
    picked_values = stored_values[slot_block, :, group_ids, :]
    packed = jnp.concatenate([picked_keys, picked_values], axis=-1)
    scale_pack = jnp.stack(
        [block_key_scales[:, 0][slot_block, group_ids], value_scales[:, 0][slot_block, group_ids]],
        axis=-1,
    )
    got_blocks, got_scales = (
        lax.all_to_all(packed, "seq", split_axis=0, concat_axis=0, tiled=True),
        lax.all_to_all(scale_pack, "seq", split_axis=0, concat_axis=0, tiled=True),
    )
    own_lists = jnp.transpose(selections[:, 0], (1, 0, 2)).reshape(groups_here, item_count)
    own_owner = own_lists % seq_count
    item_ids = jnp.arange(item_count, dtype=jnp.int32)
    earlier = (own_owner[:, :, None] == own_owner[:, None, :]) & (
        item_ids[None, None, :] < item_ids[None, :, None]
    )
    slot_of = jnp.sum(earlier.astype(jnp.int32), axis=2)
    group_rows = jnp.arange(groups_here, dtype=jnp.int32)[:, None]
    fetched_kv = got_blocks[own_owner, group_rows, slot_of]
    fetched_sc = got_scales[own_owner, group_rows, slot_of]
    inter_rank = lax.axis_index("inter")
    all_kv, all_sc = (
        lax.all_gather(fetched_kv, "inter", axis=0, tiled=True),
        lax.all_gather(fetched_sc, "inter", axis=0, tiled=True),
    )
    all_lists = lax.all_gather(selections, "inter", axis=2, tiled=True)
    whole_keys, whole_values = (
        lax.all_gather(span_keys, "inter", axis=3, tiled=True),
        lax.all_gather(span_values, "inter", axis=3, tiled=True),
    )
    group_total = all_kv.shape[0]
    row_count = queries.shape[2]
    positions = inter_rank * row_count + jnp.arange(row_count, dtype=jnp.int32)
    query_all = queries[:, 0].reshape(blocks_here, row_count, group_total, HG, DH)
    keys_all = whole_keys[:, 0].reshape(blocks_here, BLK, group_total, DH)
    values_all = whole_values[:, 0].reshape(blocks_here, BLK, group_total, DH)
    pack_all = jnp.transpose(
        all_kv.reshape(group_total, blocks_here, 3, BLK, 2 * DH), (1, 0, 2, 3, 4)
    )
    scale_all = jnp.transpose(all_sc.reshape(group_total, blocks_here, 3, 2), (1, 0, 2, 3))
    ids_all = all_lists[:, 0]

    def attend_block(inputs):
        query_vector, keys_one, values_one, pack_one, scale_one, ids_one = inputs

        def group_results(query_g, keys_g, values_g, pack_g, scale_g, ids_g):
            return attend(
                query_g,
                keys_g,
                values_g,
                pack_g[..., :DH],
                pack_g[..., DH:],
                scale_g[:, 0],
                scale_g[:, 1],
                ids_g,
                cutoff,
                positions,
            )

        return jax.vmap(group_results, in_axes=(1, 1, 1, 0, 0, 0), out_axes=1)(
            query_vector, keys_one, values_one, pack_one, scale_one, ids_one
        )

    result = lax.map(attend_block, (query_all, keys_all, values_all, pack_all, scale_all, ids_all))
    return result.reshape(blocks_here, 1, row_count, group_total * HG * DH)


def path_tables():
    def move(node, way):
        z, x = divmod(node, SIDE)
        dz, dx = ((0, 1), (0, -1), (1, 0), (-1, 0))[way]
        return (z + dz) % SIDE * SIDE + (x + dx) % SIDE

    def paths(here, there):
        if here == there:
            return [[]]
        z, x = divmod(here, SIDE)
        tz, tx = divmod(there, SIDE)
        rx, rz = (tx - x) % SIDE, (tz - z) % SIDE
        ways = [w for w, ok in enumerate((rx in (1, 2), rx in (2, 3), rz in (1, 2), rz in (2, 3))) if ok]
        return [[here * 4 + w] + rest for w in ways for rest in paths(move(here, w), there)]

    table = np.zeros((NODES * NODES, CANDS, 4), np.int32)
    dist = np.zeros((NODES * NODES,), np.int32)
    for owner in range(NODES):
        for dest in range(NODES):
            found = paths(owner, dest)
            pair = owner * NODES + dest
            dist[pair] = len(found[0])
            count = min(CANDS, len(found))
            for c in range(count):
                path = found[c * len(found) // count]
                table[pair, c, : len(path)] = path
    slot_of = np.zeros((256,), np.int32)
    for bit in range(8):
        slot_of[1 << bit] = bit
    return np.concatenate([table.reshape(-1), dist, slot_of])


TABLES = path_tables()
DIST_AT = NODES * NODES * CANDS * 4
SLOT_AT = DIST_AT + NODES * NODES
CHOICES = {4: CANDS, 3: 6, 2: 2, 1: 1}


def lists_kernel(x_ref, f_ref, i_ref, buf, send_sem, recv_sem):
    s, r = lax.axis_index("seq"), lax.axis_index("inter")
    barrier = pltpu.get_barrier_semaphore()
    for k in range(1, NODES):
        pl.semaphore_signal(
            barrier, inc=1, device_id=(lax.rem(s + k, NODES), r), device_id_type=MESH
        )
    pl.semaphore_wait(barrier, NODES - 1)
    copies = []
    for k in range(1, NODES):
        copy = pltpu.make_async_remote_copy(
            src_ref=x_ref,
            dst_ref=buf.at[s],
            send_sem=send_sem.at[k],
            recv_sem=recv_sem.at[k],
            device_id=(lax.rem(s + k, NODES), r),
            device_id_type=MESH,
        )
        copy.start()
        copies.append(copy)
    buf[s] = x_ref[...]
    for copy in copies:
        copy.wait()
    got = buf[...]
    f_ref[...] = got
    i_ref[...] = got.astype(jnp.int32)


def plan_kernel(
    lists, scales, start, tab, send, place, limit, factor, flag, occ, bucket, cnt, tbl, posn
):
    me = lax.axis_index("seq")

    def clear(i, _):
        occ[i] = 0
        return 0

    lax.fori_loop(0, NODES * 4, clear, 0, unroll=8)
    for i in range(9):
        cnt[i] = 0
    for t in range(SLOTS):
        for d in range(4):
            tbl[(me * 4 + d) * 8 + t] = 0

    def sort_dest(dest, _):
        for jk in range(6):
            block = lists[dest, 0, 64 + jk]
            owner = block & (NODES - 1)
            steps = tab[DIST_AT + owner * NODES + dest]
            posn[dest * 8 + jk] = block >> 4
            kind = jnp.where(steps == 0, 8, (jk // 3) * 4 + 4 - steps)
            at = cnt[kind]
            bucket[kind * 48 + at] = dest * 8 + jk
            cnt[kind] = at + 1
        return 0

    lax.fori_loop(0, NODES, sort_dest, 0)

    def chain(base, hops):
        links, marks = [], []
        seen = None
        for h in range(hops):
            link = tab[base + h]
            used = occ[link]
            if seen is not None:
                used = used | seen
            mark = (~used) & (used + 1)
            seen = mark | (mark - 1)
            links.append(link)
            marks.append(mark)
        return links, marks

    over = jnp.int32(0)
    for j in range(2):
        bound = 1 << (SLOTS_FIRST if j == 0 else SLOTS)
        for hops in (4, 3, 2, 1):
            kind = j * 4 + 4 - hops

            def route(i, over, kind=kind, hops=hops, bound=bound):
                item = bucket[kind * 48 + i]
                dest = item >> 3
                block = lists[dest, 0, 64 + (item & 7)]
                owner = block & (NODES - 1)
                base = (owner * NODES + dest) * (CANDS * 4)
                best_at, best = base, None
                for c in range(CHOICES[hops]):
                    cost = chain(base + 4 * c, hops)[1][-1]
                    if best is None:
                        best = cost
                    else:
                        best_at = jnp.where(cost < best, base + 4 * c, best_at)
                        best = jnp.minimum(cost, best)
                fits = best < bound

                @pl.when(fits)
                def _():
                    links, marks = chain(best_at, hops)
                    source = block >> 4
                    for link, mark in zip(links, marks):
                        occ[link] = occ[link] | mark
                        slot = tab[SLOT_AT + mark]
                        tbl[link * 8 + slot] = source
                        source = ROWS_KV + 4 * slot + (link & 3)
                    posn[item] = source

                return over | jnp.where(fits, 0, 1)

            over = lax.fori_loop(0, cnt[kind], route, over)

    for t in range(SLOTS):
        for d in range(4):
            send[t * 4 + d] = tbl[(me * 4 + d) * 8 + t]
    for jk in range(6):
        block = lists[me, 0, 64 + jk]
        owner = block & (NODES - 1)
        row = block >> 4
        place[jk] = posn[me * 8 + jk]
        limit[jk] = start[0] - block * BLK
        factor[jk] = scales[owner, 0, row] * (LOG2E / math.sqrt(DH))
        factor[8 + jk] = scales[owner, 0, ROWS_KV + row]
    flag[...] = jnp.full((1, 128), over, jnp.int32).astype(jnp.float32)


def main_kernel(
    send, place, limit, factor, flag, q, sk_hbm, sv_hbm, ck_hbm, cv_hbm,
    out, over,
    kp, vp, snd, rcv, qb, ob, sk, sv, acc, top, flags,
    load_sem, kv_send, kv_recv, q_send, q_recv, o_send, o_recv, f_send, f_recv,
):
    s, r = lax.axis_index("seq"), lax.axis_index("inter")
    z, x = s // SIDE, s % SIDE
    y, core = r // 2, r % 2
    beside = (
        z * SIDE + (x + 1) % SIDE,
        z * SIDE + (x + 3) % SIDE,
        (z + 1) % SIDE * SIDE + x,
        (z + 3) % SIDE * SIDE + x,
    )

    def peer(k):
        pair = k // 2
        dy = (2 + 3 * pair + 3 * (pair * (pair - 1) // 2)) % 4
        return (y + dy) % 4 * 2 + (core + 1 + k) % 2

    loads = [
        pltpu.make_async_copy(ck_hbm.at[:, 0], kp.at[pl.ds(0, ROWS_KV)], load_sem.at[0]),
        pltpu.make_async_copy(cv_hbm.at[:, 0], vp.at[pl.ds(0, ROWS_KV)], load_sem.at[1]),
        pltpu.make_async_copy(sk_hbm.at[:, 0], sk, load_sem.at[2]),
        pltpu.make_async_copy(sv_hbm.at[:, 0], sv, load_sem.at[3]),
        pltpu.make_async_copy(
            q.at[:, 0, :, pl.ds(pl.multiple_of(r * WIDE, WIDE), WIDE)],
            qb.at[:, pl.ds(pl.multiple_of(r * QROWS, QROWS), QROWS)],
            load_sem.at[4],
        ),
    ]
    for load in loads:
        load.start()

    barrier = pltpu.get_barrier_semaphore()
    for n in beside:
        pl.semaphore_signal(barrier, inc=1, device_id=(n, r), device_id_type=MESH)
    for k in range(PEERS - 1):
        pl.semaphore_signal(barrier, inc=1, device_id=(s, peer(k)), device_id_type=MESH)
    pl.semaphore_wait(barrier, PEERS + 3)

    def kv_copy(t, d, h):
        return pltpu.make_async_remote_copy(
            src_ref=snd.at[t, d, h],
            dst_ref=rcv.at[t, d, h],
            send_sem=kv_send.at[t, d, h],
            recv_sem=kv_recv.at[t, d, h],
            device_id=(beside[d], r),
            device_id_type=MESH,
        )

    def q_copy(k):
        to = peer(k)
        return pltpu.make_async_remote_copy(
            src_ref=q.at[:, 0, :, pl.ds(pl.multiple_of(to * WIDE, WIDE), WIDE)],
            dst_ref=qb.at[:, pl.ds(pl.multiple_of(r * QROWS, QROWS), QROWS)],
            send_sem=q_send.at[k],
            recv_sem=q_recv.at[k],
            device_id=(s, to),
            device_id_type=MESH,
        )

    def f_copy(k):
        return pltpu.make_async_remote_copy(
            src_ref=flag,
            dst_ref=flags.at[r],
            send_sem=f_send.at[k],
            recv_sem=f_recv.at[k],
            device_id=(s, peer(k)),
            device_id_type=MESH,
        )

    def o_copy(j, k):
        to = peer(k)
        return pltpu.make_async_remote_copy(
            src_ref=ob.at[j, pl.ds(pl.multiple_of(to * QROWS, QROWS), QROWS)],
            dst_ref=out.at[j, 0, :, pl.ds(pl.multiple_of(r * WIDE, WIDE), WIDE)],
            send_sem=o_send.at[j, k],
            recv_sem=o_recv.at[j, k],
            device_id=(s, to),
            device_id_type=MESH,
        )

    def o_own(j):
        return pltpu.make_async_copy(
            ob.at[j, pl.ds(pl.multiple_of(r * QROWS, QROWS), QROWS)],
            out.at[j, 0, :, pl.ds(pl.multiple_of(r * WIDE, WIDE), WIDE)],
            load_sem.at[5 + j],
        )

    def pump(t, h):
        pool = (kp, vp)[h]
        if t > 0:
            for d in range(4):
                kv_copy(t - 1, d, h).wait_recv()
            for d in range(4):
                pool[ROWS_KV + 4 * (t - 1) + d] = rcv[t - 1, d, h]
        if t < SLOTS:
            for d in range(4):
                snd[t, d, h] = pool[send[t * 4 + d]]
                kv_copy(t, d, h).start()

    def rows_of(c):
        return pl.ds(pl.multiple_of(c * QROWS, QROWS), QROWS)

    def load_q(j, c):
        tile = qb[j, rows_of(c), :]
        return jnp.concatenate([tile[:, h * DH : (h + 1) * DH] for h in range(HG)], axis=0)

    def scores_of(query, keys):
        return lax.dot_general(
            query, keys, (((1,), (1,)), ((), ())), preferred_element_type=jnp.float32
        )

    ones = jnp.ones((BLK, DH), jnp.bfloat16)
    column = lax.broadcasted_iota(jnp.int32, (1, BLK), 1)

    def own_tile(j, c):
        scores = scores_of(load_q(j, c), sk[j]) * (LOG2E / math.sqrt(DH))
        row = lax.broadcasted_iota(jnp.int32, (TILE_ROWS, 1), 0) % QROWS + c * QROWS
        scores = jnp.where(column <= row, scores, NEG)
        high = jnp.max(scores, axis=1, keepdims=True)
        weights = jnp.exp2(scores - high).astype(jnp.bfloat16)
        acc[j, c] = jnp.dot(
            weights, jnp.concatenate([sv[j], ones], axis=1), preferred_element_type=jnp.float32
        )
        top[j, c] = jnp.broadcast_to(high, (TILE_ROWS, DH))

    def cache_tile(j, c):
        query = load_q(j, c)
        before = top[j, c][:, :1]
        parts = []
        high = before
        for i in range(3 * j, 3 * j + 3):
            bias = jnp.where(column < limit[i], 0.0, NEG)
            part = scores_of(query, kp[place[i]]) * factor[i] + bias
            high = jnp.maximum(high, jnp.max(part, axis=1, keepdims=True))
            parts.append(part)
        fade = jnp.exp2(before - high)
        old = acc[j, c]
        summed = old[:, :DH] * fade
        total = old[:, DH:] * fade
        for i, part in zip(range(3 * j, 3 * j + 3), parts):
            weights = jnp.exp2(part - high).astype(jnp.bfloat16)
            more = jnp.dot(
                weights,
                jnp.concatenate([vp[place[i]], ones], axis=1),
                preferred_element_type=jnp.float32,
            )
            summed = summed + more[:, :DH] * factor[8 + i]
            total = total + more[:, DH:]
        done = (summed / total).astype(jnp.bfloat16)
        for h in range(HG):
            ob[j, rows_of(c), h * DH : (h + 1) * DH] = done[h * QROWS : (h + 1) * QROWS]

    def own_block(j):
        def step(c, _):
            own_tile(j, c)
            return 0

        lax.fori_loop(0, PEERS, step, 0)

    def cache_blocks(j):
        def step(k, _):
            cache_tile(j, peer(k))
            o_copy(j, k).start()
            return 0

        lax.fori_loop(0, PEERS - 1, step, 0)
        cache_tile(j, r)
        o_own(j).start()

    for k in range(PEERS - 1):
        q_copy(k).start()
    loads[0].wait()
    pump(0, 0)
    loads[1].wait()
    pump(0, 1)
    for k in range(PEERS - 1):
        f_copy(k).start()
    flags[r] = flag[...]
    for load in loads[2:]:
        load.wait()
    for t in range(1, SLOTS + 1):
        for h in range(2):
            pump(t, h)
            if (t, h) == (3, 0):
                for k in range(PEERS - 1):
                    q_copy(k).wait()
                own_block(0)
            if (t, h) == (4, 0):
                own_block(1)
            if (t, h) == (SLOTS_FIRST, 1):
                cache_blocks(0)
    cache_blocks(1)
    for k in range(PEERS - 1):
        f_copy(k).wait()
    worst = flags[0]
    for k in range(1, PEERS):
        worst = jnp.maximum(worst, flags[k])
    over[...] = worst
    for t in range(SLOTS):
        for d in range(4):
            for h in range(2):
                kv_copy(t, d, h).wait_send()
    for j in range(2):
        o_own(j).wait()
        for k in range(PEERS - 1):
            o_copy(j, k).wait()


def routed(
    queries, span_keys, span_values, cache_keys, cache_values, key_scales, value_scales, selections, start
):
    f32, i32, bf16 = jnp.float32, jnp.int32, jnp.bfloat16
    smem = pl.BlockSpec(memory_space=pltpu.SMEM)
    vmem = pl.BlockSpec(memory_space=pltpu.VMEM)
    hbm = pl.BlockSpec(memory_space=pl.ANY)
    dma = pltpu.SemaphoreType.DMA
    row = jnp.concatenate(
        [key_scales.reshape(-1).astype(f32), value_scales.reshape(-1).astype(f32), selections.reshape(-1).astype(f32)]
    )
    row = jnp.pad(row, (0, 128 - row.shape[0])).reshape(1, 128)
    scales, lists = pl.pallas_call(
        lists_kernel,
        out_shape=(
            jax.ShapeDtypeStruct((NODES, 1, 128), f32),
            jax.ShapeDtypeStruct((NODES, 1, 128), i32),
        ),
        in_specs=[vmem],
        out_specs=(vmem, vmem),
        scratch_shapes=[pltpu.VMEM((NODES, 1, 128), f32), dma((NODES,)), dma((NODES,))],
        compiler_params=pltpu.CompilerParams(collective_id=0, has_side_effects=True),
        name="lists",
    )(row)
    send, place, limit, factor, flag = pl.pallas_call(
        plan_kernel,
        out_shape=(
            jax.ShapeDtypeStruct((4 * SLOTS,), i32),
            jax.ShapeDtypeStruct((8,), i32),
            jax.ShapeDtypeStruct((8,), i32),
            jax.ShapeDtypeStruct((16,), f32),
            jax.ShapeDtypeStruct((1, 128), f32),
        ),
        in_specs=[smem] * 4,
        out_specs=(smem, smem, smem, smem, vmem),
        scratch_shapes=[
            pltpu.SMEM((NODES * 4,), i32),
            pltpu.SMEM((9 * 48 + 96,), i32),
            pltpu.SMEM((16,), i32),
            pltpu.SMEM((NODES * 4 * 8,), i32),
            pltpu.SMEM((NODES * 8,), i32),
        ],
        name="plan",
    )(lists, scales, start, jnp.asarray(TABLES))
    return pl.pallas_call(
        main_kernel,
        out_shape=(
            jax.ShapeDtypeStruct(queries.shape, bf16),
            jax.ShapeDtypeStruct((1, 128), f32),
        ),
        in_specs=[smem] * 4 + [vmem] + [hbm] * 5,
        out_specs=(hbm, vmem),
        scratch_shapes=[
            pltpu.VMEM((POOL, BLK, DH), bf16),
            pltpu.VMEM((POOL, BLK, DH), bf16),
            pltpu.VMEM((SLOTS, 4, 2, BLK, DH), bf16),
            pltpu.VMEM((SLOTS, 4, 2, BLK, DH), bf16),
            pltpu.VMEM((2, BLK, WIDE), bf16),
            pltpu.VMEM((2, BLK, WIDE), bf16),
            pltpu.VMEM((2, BLK, DH), bf16),
            pltpu.VMEM((2, BLK, DH), bf16),
            pltpu.VMEM((2, PEERS, TILE_ROWS, 2 * DH), f32),
            pltpu.VMEM((2, PEERS, TILE_ROWS, DH), f32),
            pltpu.VMEM((PEERS, 1, 128), f32),
            dma((8,)),
            dma((SLOTS, 4, 2)),
            dma((SLOTS, 4, 2)),
            dma((PEERS,)),
            dma((PEERS,)),
            dma((2, PEERS)),
            dma((2, PEERS)),
            dma((PEERS,)),
            dma((PEERS,)),
        ],
        compiler_params=pltpu.CompilerParams(
            collective_id=1, has_side_effects=True, vmem_limit_bytes=56 * 2**20
        ),
        name="exchange_attend",
    )(send, place, limit, factor, flag, queries, span_keys, span_values, cache_keys, cache_values)


def per_device(*arrays):
    attended, over = routed(*arrays)
    return lax.cond(over[0, 0] > 0, lambda: exchange_all(*arrays), lambda: attended)


def solution(mesh):
    placed = (
        P(None, "seq", "inter", None),
        P(None, "seq", None, "inter"),
        P(None, "seq", None, "inter"),
        P(None, "seq", None, "inter"),
        P(None, "seq", None, "inter"),
        P(None, "seq", "inter"),
        P(None, "seq", "inter"),
        P(None, "seq", "inter", None),
        P(),
    )
    return jax.shard_map(
        per_device,
        mesh=mesh,
        in_specs=placed,
        out_specs=P(None, "seq", "inter", None),
        check_vma=False,
    )
```

```python
import functools
import math

import jax
import jax.numpy as jnp
import numpy as np
from jax import lax
from jax.experimental import pallas as pl
from jax.experimental.pallas import tpu as pltpu
from jax.sharding import PartitionSpec as P

DH = 128
BLK = 512
HG = 4
SIDE = 4
NODES = SIDE * SIDE
ROWS_KV = 32
SLOTS = 6
SLOTS_FIRST = 5
CANDS = 8
TRIES = 10
LOAD = 256
PEERS = 8
QROWS = BLK // PEERS
WIDE = HG * DH
TILE_ROWS = HG * QROWS
POOL = ROWS_KV + 4 * SLOTS
LOG2E = 1.4426950408889634
NEG = -1e30
MESH = pl.DeviceIdType.MESH


def attend(
    query_vector,
    own_keys,
    own_values,
    chosen_keys,
    chosen_values,
    key_scale,
    value_scale,
    sel_blocks,
    cutoff,
    positions,
):
    row_count = query_vector.shape[0]
    head_count = query_vector.shape[1]
    head_dim = query_vector.shape[2]
    block_len = own_keys.shape[0]
    all_keys = jnp.concatenate([own_keys, chosen_keys.reshape(-1, head_dim)], axis=0)
    flat_query = query_vector.reshape(row_count * head_count, head_dim)
    scores = lax.dot_general(
        flat_query, all_keys, (((1,), (1,)), ((), ())), preferred_element_type=jnp.float32
    )
    column_scale = jnp.concatenate(
        [jnp.ones((block_len,), jnp.float32), jnp.repeat(key_scale.astype(jnp.float32), block_len)]
    )
    scores = scores * (column_scale / math.sqrt(head_dim))
    scores = scores.reshape(row_count, head_count, -1)
    key_index = jnp.arange(block_len, dtype=jnp.int32)
    own_ok = positions[:, None] >= key_index[None, :]
    sel_ok = (sel_blocks[:, None] * block_len + key_index[None, :] < cutoff).reshape(-1)
    allowed = jnp.concatenate(
        [own_ok, jnp.broadcast_to(sel_ok[None, :], (row_count, sel_ok.shape[0]))], axis=1
    )[:, None, :]
    top_score = jnp.max(jnp.where(allowed, scores, -jnp.inf), axis=-1, keepdims=True)
    weights = jnp.where(allowed, jnp.exp(jnp.where(allowed, scores, top_score) - top_score), 0.0)
    total = jnp.sum(weights, axis=-1, keepdims=True)
    rounded = weights.astype(jnp.bfloat16).reshape(row_count * head_count, -1)
    summed = jnp.dot(rounded[:, :block_len], own_values, preferred_element_type=jnp.float32)
    for index in range(chosen_values.shape[0]):
        piece = rounded[:, (index + 1) * block_len : (index + 2) * block_len]
        summed = summed + value_scale[index].astype(jnp.float32) * jnp.dot(
            piece, chosen_values[index], preferred_element_type=jnp.float32
        )
    return (summed.reshape(row_count, head_count, head_dim) / total).astype(jnp.bfloat16)


def padded(queries, span_keys, span_values, cache_keys, cache_values, start, lists, scales):
    blocks_here = queries.shape[0]
    seq_rank = lax.axis_index("seq")
    wanted = lists[:, 0, 64:70]
    owner_rank = wanted % NODES
    local_row = wanted // NODES
    is_mine = (owner_rank == seq_rank).astype(jnp.int32)
    ranking = jnp.cumsum(is_mine, axis=1) - 1
    slot_ids = jnp.arange(2, dtype=jnp.int32)
    slot_hits = (is_mine[..., None] == 1) & (ranking[..., None] == slot_ids)
    slot_block = jnp.sum(jnp.where(slot_hits, local_row[..., None], 0), axis=1)
    packed = jnp.concatenate([cache_keys[slot_block, 0], cache_values[slot_block, 0]], axis=-1)
    got_blocks = lax.all_to_all(packed, "seq", split_axis=0, concat_axis=0, tiled=True)
    own_list = wanted[seq_rank]
    own_owner = own_list % NODES
    item_ids = jnp.arange(6, dtype=jnp.int32)
    earlier = (own_owner[:, None] == own_owner[None, :]) & (item_ids[None, :] < item_ids[:, None])
    slot_of = jnp.sum(earlier.astype(jnp.int32), axis=1)
    fetched = got_blocks[own_owner, slot_of].reshape(blocks_here, 3, BLK, 2 * DH)
    row = own_list // NODES
    key_scale = scales[own_owner, 0, row].reshape(blocks_here, 3)
    value_scale = scales[own_owner, 0, ROWS_KV + row].reshape(blocks_here, 3)
    whole = lax.all_to_all(queries, "inter", split_axis=3, concat_axis=2, tiled=True)
    positions = jnp.arange(BLK, dtype=jnp.int32)

    def attend_block(inputs):
        query, keys, values, pack, key_scale, value_scale, ids = inputs
        return attend(
            query, keys, values, pack[..., :DH], pack[..., DH:], key_scale, value_scale, ids, start[0], positions
        )

    result = lax.map(
        attend_block,
        (
            whole.reshape(blocks_here, BLK, HG, DH),
            span_keys[:, 0],
            span_values[:, 0],
            fetched,
            key_scale,
            value_scale,
            own_list.reshape(blocks_here, 3),
        ),
    )
    result = result.reshape(blocks_here, 1, BLK, WIDE)
    return lax.all_to_all(result, "inter", split_axis=2, concat_axis=3, tiled=True)


def path_tables():
    def move(node, way):
        z, x = divmod(node, SIDE)
        dz, dx = ((0, 1), (0, -1), (1, 0), (-1, 0))[way]
        return (z + dz) % SIDE * SIDE + (x + dx) % SIDE

    def paths(here, there):
        if here == there:
            return [[]]
        z, x = divmod(here, SIDE)
        tz, tx = divmod(there, SIDE)
        rx, rz = (tx - x) % SIDE, (tz - z) % SIDE
        ways = [w for w, ok in enumerate((rx in (1, 2), rx in (2, 3), rz in (1, 2), rz in (2, 3))) if ok]
        return [[here * 4 + w] + rest for w in ways for rest in paths(move(here, w), there)]

    table = np.zeros((NODES * NODES, CANDS, 4), np.int32)
    dist = np.zeros((NODES * NODES,), np.int32)
    for owner in range(NODES):
        for dest in range(NODES):
            found = paths(owner, dest)
            pair = owner * NODES + dest
            dist[pair] = len(found[0])
            count = min(6, len(found))
            for c in range(count):
                path = found[c * len(found) // count]
                table[pair, c, : len(path)] = path
    slot_of = np.zeros((256,), np.int32)
    for bit in range(8):
        slot_of[(2 << bit) - 1] = bit
    return np.concatenate([table.reshape(-1), dist, slot_of])


TABLES = path_tables()
DIST_AT = NODES * NODES * CANDS * 4
SLOT_AT = DIST_AT + NODES * NODES
CHOICES = {4: 6, 3: 6, 2: 2, 1: 1}


def lists_kernel(ks_ref, vs_ref, sel_ref, f_ref, i_ref, x_ref, buf, send_sem, recv_sem):
    s, r = lax.axis_index("seq"), lax.axis_index("inter")
    barrier = pltpu.get_barrier_semaphore()
    for k in range(1, NODES):
        pl.semaphore_signal(
            barrier, inc=1, device_id=(lax.rem(s + k, NODES), r), device_id_type=MESH
        )
    x_ref[...] = jnp.zeros_like(x_ref)
    x_ref[0:1, 0:ROWS_KV] = ks_ref[...].astype(jnp.float32)
    x_ref[0:1, ROWS_KV : 2 * ROWS_KV] = vs_ref[...].astype(jnp.float32)
    for j in range(2):
        x_ref[0:1, 64 + 3 * j : 67 + 3 * j] = sel_ref[j : j + 1].astype(jnp.float32)
    pl.semaphore_wait(barrier, NODES - 1)
    copies = []
    for k in range(1, NODES):
        copy = pltpu.make_async_remote_copy(
            src_ref=x_ref,
            dst_ref=buf.at[s],
            send_sem=send_sem.at[k],
            recv_sem=recv_sem.at[k],
            device_id=(lax.rem(s + k, NODES), r),
            device_id_type=MESH,
        )
        copy.start()
        copies.append(copy)
    buf[s] = x_ref[...]
    for copy in copies:
        copy.wait()
    got = buf[...]
    f_ref[...] = got
    i_ref[...] = got.astype(jnp.int32)


def plan_kernel(
    lists, scales, start, tab, send, place, limit, factor, flag, occ, bucket, cnt, tbl, posn, front
):
    me = lax.axis_index("seq")

    def clear(ref, count):
        def step(i, _):
            ref[i] = 0
            return 0

        lax.fori_loop(0, count, step, 0, unroll=8)

    clear(front, NODES * 8)
    for t in range(SLOTS):
        for d in range(4):
            tbl[(me * 4 + d) * 8 + t] = 0

    def sort_dest(dest, _):
        for jk in range(6):
            block = lists[dest, 0, 64 + jk]
            owner = block & (NODES - 1)
            steps = tab[DIST_AT + owner * NODES + dest]
            item = dest * 8 + jk
            posn[item] = block >> 4
            phase = jnp.where(front[item] > 0, 0, 1 + jk // 3)
            kind = jnp.where(steps == 0, 12, phase * 4 + 4 - steps)
            at = cnt[kind]
            bucket[kind * 96 + at] = item
            cnt[kind] = at + 1
        return 0

    def chain(base, hops):
        links, ends = [], []
        seen, words = 0, 0
        for h in range(hops):
            link = tab[base + h]
            word = occ[link]
            used = word | seen
            seen = used ^ (used + 1)
            words = words + word
            links.append(link)
            ends.append(seen)
        return links, ends, words

    def attempt(carry):
        clear(occ, NODES * 4)
        for kind in range(13):
            cnt[kind] = 0
        lax.fori_loop(0, NODES, sort_dest, 0)

        def run_phase(phase, missed):
            for hops in (4, 3, 2, 1):
                kind = phase * 4 + 4 - hops

                def route(i, missed, kind=kind, hops=hops):
                    item = bucket[kind * 96 + i]
                    dest = item >> 3
                    jk = item & 7
                    block = lists[dest, 0, 64 + jk]
                    owner = block & (NODES - 1)
                    base = (owner * NODES + dest) * (CANDS * 4)
                    best_at, best = base, None
                    for c in range(CHOICES[hops]):
                        _, ends, words = chain(base + 4 * c, hops)
                        cost = (ends[-1] << 16) + words
                        if best is None:
                            best = cost
                        else:
                            best_at = jnp.where(cost < best, base + 4 * c, best_at)
                            best = jnp.minimum(cost, best)
                    fits = best < jnp.where(jk < 3, 1 << (16 + SLOTS_FIRST), 1 << (16 + SLOTS))

                    @pl.when(fits)
                    def _():
                        links, ends, _ = chain(best_at, hops)
                        source = block >> 4
                        for link, end in zip(links, ends):
                            occ[link] = (occ[link] | ((end + 1) >> 1)) + LOAD
                            slot = tab[SLOT_AT + end]
                            tbl[link * 8 + slot] = source
                            source = ROWS_KV + 4 * slot + (link & 3)
                        posn[item] = source

                    @pl.when(jnp.logical_not(fits))
                    def _():
                        front[item] = 1

                    return missed + jnp.where(fits, 0, 1)

                missed = lax.fori_loop(0, cnt[kind], route, missed)
            return missed

        return lax.fori_loop(0, 3, run_phase, jnp.int32(0)), carry[1] + 1

    missed, _ = lax.while_loop(
        lambda carry: (carry[0] > 0) & (carry[1] < TRIES), attempt, (jnp.int32(1), jnp.int32(0))
    )
    for t in range(SLOTS):
        for d in range(4):
            send[t * 4 + d] = tbl[(me * 4 + d) * 8 + t]
    for jk in range(6):
        block = lists[me, 0, 64 + jk]
        owner = block & (NODES - 1)
        row = block >> 4
        place[jk] = posn[me * 8 + jk]
        limit[jk] = start[0] - block * BLK
        factor[jk] = scales[owner, 0, row] * (LOG2E / math.sqrt(DH))
        factor[8 + jk] = scales[owner, 0, ROWS_KV + row]
    flag[...] = jnp.full((1, 128), missed, jnp.int32).astype(jnp.float32)


def main_kernel(
    send, place, limit, factor, flag, q, sk_hbm, sv_hbm, ck_hbm, cv_hbm,
    out, over,
    kp, vp, snd, rcv, qb, ob, sk, sv, acc, top, flags,
    load_sem, kv_send, kv_recv, q_send, q_recv, o_send, o_recv, f_send, f_recv,
):
    s, r = lax.axis_index("seq"), lax.axis_index("inter")
    z, x = s // SIDE, s % SIDE
    y, core = r // 2, r % 2
    beside = (
        z * SIDE + (x + 1) % SIDE,
        z * SIDE + (x + 3) % SIDE,
        (z + 1) % SIDE * SIDE + x,
        (z + 3) % SIDE * SIDE + x,
    )

    def peer(k):
        pair = k // 2
        dy = (2 + 3 * pair + 3 * (pair * (pair - 1) // 2)) % 4
        return (y + dy) % 4 * 2 + (core + 1 + k) % 2

    loads = [
        pltpu.make_async_copy(ck_hbm.at[:, 0], kp.at[pl.ds(0, ROWS_KV)], load_sem.at[0]),
        pltpu.make_async_copy(cv_hbm.at[:, 0], vp.at[pl.ds(0, ROWS_KV)], load_sem.at[1]),
        pltpu.make_async_copy(sk_hbm.at[:, 0], sk, load_sem.at[2]),
        pltpu.make_async_copy(sv_hbm.at[:, 0], sv, load_sem.at[3]),
        pltpu.make_async_copy(
            q.at[:, 0, :, pl.ds(pl.multiple_of(r * WIDE, WIDE), WIDE)],
            qb.at[:, pl.ds(pl.multiple_of(r * QROWS, QROWS), QROWS)],
            load_sem.at[4],
        ),
    ]
    for load in loads:
        load.start()

    barrier = pltpu.get_barrier_semaphore()
    for n in beside:
        pl.semaphore_signal(barrier, inc=1, device_id=(n, r), device_id_type=MESH)
    for k in range(PEERS - 1):
        pl.semaphore_signal(barrier, inc=1, device_id=(s, peer(k)), device_id_type=MESH)
    pl.semaphore_wait(barrier, PEERS + 3)

    def kv_copy(t, d, h):
        return pltpu.make_async_remote_copy(
            src_ref=snd.at[t, d, h],
            dst_ref=rcv.at[t, d, h],
            send_sem=kv_send.at[t, d, h],
            recv_sem=kv_recv.at[t, d, h],
            device_id=(beside[d], r),
            device_id_type=MESH,
        )

    def q_copy(k):
        to = peer(k)
        return pltpu.make_async_remote_copy(
            src_ref=q.at[:, 0, :, pl.ds(pl.multiple_of(to * WIDE, WIDE), WIDE)],
            dst_ref=qb.at[:, pl.ds(pl.multiple_of(r * QROWS, QROWS), QROWS)],
            send_sem=q_send.at[k],
            recv_sem=q_recv.at[k],
            device_id=(s, to),
            device_id_type=MESH,
        )

    def f_copy(k):
        return pltpu.make_async_remote_copy(
            src_ref=flag,
            dst_ref=flags.at[r],
            send_sem=f_send.at[k],
            recv_sem=f_recv.at[k],
            device_id=(s, peer(k)),
            device_id_type=MESH,
        )

    def o_copy(j, k):
        to = peer(k)
        return pltpu.make_async_remote_copy(
            src_ref=ob.at[j, pl.ds(pl.multiple_of(to * QROWS, QROWS), QROWS)],
            dst_ref=out.at[j, 0, :, pl.ds(pl.multiple_of(r * WIDE, WIDE), WIDE)],
            send_sem=o_send.at[j, k],
            recv_sem=o_recv.at[j, k],
            device_id=(s, to),
            device_id_type=MESH,
        )

    def o_own(j):
        return pltpu.make_async_copy(
            ob.at[j, pl.ds(pl.multiple_of(r * QROWS, QROWS), QROWS)],
            out.at[j, 0, :, pl.ds(pl.multiple_of(r * WIDE, WIDE), WIDE)],
            load_sem.at[5 + j],
        )

    def pump(t, h):
        pool = (kp, vp)[h]
        if t > 0:
            for d in range(4):
                kv_copy(t - 1, d, h).wait_recv()
            for d in range(4):
                pool[ROWS_KV + 4 * (t - 1) + d] = rcv[t - 1, d, h]
        if t < SLOTS:
            for d in range(4):
                snd[t, d, h] = pool[send[t * 4 + d]]
                kv_copy(t, d, h).start()

    def rows_of(c):
        return pl.ds(pl.multiple_of(c * QROWS, QROWS), QROWS)

    def load_q(j, c):
        tile = qb[j, rows_of(c), :]
        return jnp.concatenate([tile[:, h * DH : (h + 1) * DH] for h in range(HG)], axis=0)

    def scores_of(query, keys):
        return lax.dot_general(
            query, keys, (((1,), (1,)), ((), ())), preferred_element_type=jnp.float32
        )

    ones = jnp.ones((BLK, DH), jnp.bfloat16)
    column = lax.broadcasted_iota(jnp.int32, (1, BLK), 1)

    def own_tile(j, c):
        scores = scores_of(load_q(j, c), sk[j]) * (LOG2E / math.sqrt(DH))
        row = lax.broadcasted_iota(jnp.int32, (TILE_ROWS, 1), 0) % QROWS + c * QROWS
        scores = jnp.where(column <= row, scores, NEG)
        high = jnp.max(scores, axis=1, keepdims=True)
        weights = jnp.exp2(scores - high).astype(jnp.bfloat16)
        acc[j, c] = jnp.dot(
            weights, jnp.concatenate([sv[j], ones], axis=1), preferred_element_type=jnp.float32
        )
        top[j, c] = jnp.broadcast_to(high, (TILE_ROWS, DH))

    def cache_tile(j, c):
        query = load_q(j, c)
        before = top[j, c][:, :1]
        parts = []
        high = before
        for i in range(3 * j, 3 * j + 3):
            bias = jnp.where(column < limit[i], 0.0, NEG)
            part = scores_of(query, kp[place[i]]) * factor[i] + bias
            high = jnp.maximum(high, jnp.max(part, axis=1, keepdims=True))
            parts.append(part)
        fade = jnp.exp2(before - high)
        old = acc[j, c]
        summed = old[:, :DH] * fade
        total = old[:, DH:] * fade
        for i, part in zip(range(3 * j, 3 * j + 3), parts):
            weights = jnp.exp2(part - high).astype(jnp.bfloat16)
            more = jnp.dot(
                weights,
                jnp.concatenate([vp[place[i]], ones], axis=1),
                preferred_element_type=jnp.float32,
            )
            summed = summed + more[:, :DH] * factor[8 + i]
            total = total + more[:, DH:]
        done = (summed / total).astype(jnp.bfloat16)
        for h in range(HG):
            ob[j, rows_of(c), h * DH : (h + 1) * DH] = done[h * QROWS : (h + 1) * QROWS]

    def own_block(j):
        def step(c, _):
            own_tile(j, c)
            return 0

        lax.fori_loop(0, PEERS, step, 0)

    def cache_blocks(j):
        def step(k, _):
            cache_tile(j, peer(k))
            o_copy(j, k).start()
            return 0

        lax.fori_loop(0, PEERS - 1, step, 0)
        cache_tile(j, r)
        o_own(j).start()

    for k in range(PEERS - 1):
        q_copy(k).start()
    loads[0].wait()
    pump(0, 0)
    loads[1].wait()
    pump(0, 1)
    for k in range(PEERS - 1):
        f_copy(k).start()
    flags[r] = flag[...]
    for load in loads[2:]:
        load.wait()
    for t in range(1, SLOTS + 1):
        for h in range(2):
            pump(t, h)
            if (t, h) == (3, 0):
                for k in range(PEERS - 1):
                    q_copy(k).wait()
                own_block(0)
            if (t, h) == (4, 0):
                own_block(1)
            if (t, h) == (SLOTS_FIRST, 1):
                cache_blocks(0)
    cache_blocks(1)
    for k in range(PEERS - 1):
        f_copy(k).wait()
    worst = flags[0]
    for k in range(1, PEERS):
        worst = jnp.maximum(worst, flags[k])
    over[...] = worst
    for t in range(SLOTS):
        for d in range(4):
            for h in range(2):
                kv_copy(t, d, h).wait_send()
    for j in range(2):
        o_own(j).wait()
        for k in range(PEERS - 1):
            o_copy(j, k).wait()


def per_device(
    queries, span_keys, span_values, cache_keys, cache_values, key_scales, value_scales, selections, start
):
    f32, i32, bf16 = jnp.float32, jnp.int32, jnp.bfloat16
    smem = pl.BlockSpec(memory_space=pltpu.SMEM)
    vmem = pl.BlockSpec(memory_space=pltpu.VMEM)
    hbm = pl.BlockSpec(memory_space=pl.ANY)
    dma = pltpu.SemaphoreType.DMA
    scales, lists = pl.pallas_call(
        lists_kernel,
        out_shape=(
            jax.ShapeDtypeStruct((NODES, 1, 128), f32),
            jax.ShapeDtypeStruct((NODES, 1, 128), i32),
        ),
        in_specs=[vmem] * 3,
        out_specs=(vmem, vmem),
        scratch_shapes=[
            pltpu.VMEM((1, 128), f32),
            pltpu.VMEM((NODES, 1, 128), f32),
            dma((NODES,)),
            dma((NODES,)),
        ],
        compiler_params=pltpu.CompilerParams(collective_id=0, has_side_effects=True),
        name="lists",
    )(key_scales.reshape(1, ROWS_KV), value_scales.reshape(1, ROWS_KV), selections.reshape(2, 3))
    send, place, limit, factor, flag = pl.pallas_call(
        plan_kernel,
        out_shape=(
            jax.ShapeDtypeStruct((4 * SLOTS,), i32),
            jax.ShapeDtypeStruct((8,), i32),
            jax.ShapeDtypeStruct((8,), i32),
            jax.ShapeDtypeStruct((16,), f32),
            jax.ShapeDtypeStruct((1, 128), f32),
        ),
        in_specs=[smem] * 4,
        out_specs=(smem, smem, smem, smem, vmem),
        scratch_shapes=[
            pltpu.SMEM((NODES * 4,), i32),
            pltpu.SMEM((13 * 96,), i32),
            pltpu.SMEM((16,), i32),
            pltpu.SMEM((NODES * 4 * 8,), i32),
            pltpu.SMEM((NODES * 8,), i32),
            pltpu.SMEM((NODES * 8,), i32),
        ],
        name="plan",
    )(lists, scales, start, jnp.asarray(TABLES))
    attended, over = pl.pallas_call(
        main_kernel,
        out_shape=(
            jax.ShapeDtypeStruct(queries.shape, bf16),
            jax.ShapeDtypeStruct((1, 128), f32),
        ),
        in_specs=[smem] * 4 + [vmem] + [hbm] * 5,
        out_specs=(hbm, vmem),
        scratch_shapes=[
            pltpu.VMEM((POOL, BLK, DH), bf16),
            pltpu.VMEM((POOL, BLK, DH), bf16),
            pltpu.VMEM((SLOTS, 4, 2, BLK, DH), bf16),
            pltpu.VMEM((SLOTS, 4, 2, BLK, DH), bf16),
            pltpu.VMEM((2, BLK, WIDE), bf16),
            pltpu.VMEM((2, BLK, WIDE), bf16),
            pltpu.VMEM((2, BLK, DH), bf16),
            pltpu.VMEM((2, BLK, DH), bf16),
            pltpu.VMEM((2, PEERS, TILE_ROWS, 2 * DH), f32),
            pltpu.VMEM((2, PEERS, TILE_ROWS, DH), f32),
            pltpu.VMEM((PEERS, 1, 128), f32),
            dma((8,)),
            dma((SLOTS, 4, 2)),
            dma((SLOTS, 4, 2)),
            dma((PEERS,)),
            dma((PEERS,)),
            dma((2, PEERS)),
            dma((2, PEERS)),
            dma((PEERS,)),
            dma((PEERS,)),
        ],
        compiler_params=pltpu.CompilerParams(
            collective_id=1, has_side_effects=True, vmem_limit_bytes=56 * 2**20
        ),
        name="exchange_attend",
    )(send, place, limit, factor, flag, queries, span_keys, span_values, cache_keys, cache_values)
    return lax.cond(
        over[0, 0] > 0,
        lambda: padded(queries, span_keys, span_values, cache_keys, cache_values, start, lists, scales),
        lambda: attended,
    )


def solution(mesh):
    placed = (
        P(None, "seq", "inter", None),
        P(None, "seq", None, "inter"),
        P(None, "seq", None, "inter"),
        P(None, "seq", None, "inter"),
        P(None, "seq", None, "inter"),
        P(None, "seq", "inter"),
        P(None, "seq", "inter"),
        P(None, "seq", "inter", None),
        P(),
    )
    return jax.shard_map(
        per_device,
        mesh=mesh,
        in_specs=placed,
        out_specs=P(None, "seq", "inter", None),
        check_vma=False,
    )
```

```python
import functools
import math

import jax
import jax.numpy as jnp
import numpy as np
from jax import lax
from jax.experimental import pallas as pl
from jax.experimental.pallas import tpu as pltpu
from jax.sharding import PartitionSpec as P

DH = 128
BLK = 512
HG = 4
SIDE = 4
NODES = SIDE * SIDE
ROWS_KV = 32
SLOTS = 6
SLOTS_FIRST = 4
CANDS = 6
TRIES = 10
LOAD = 256
PEERS = 8
QROWS = BLK // PEERS
WIDE = HG * DH
CHIPS = PEERS // 2
CROWS = 2 * QROWS
TILE_ROWS = HG * CROWS
POOL = ROWS_KV + 4 * SLOTS
LOG2E = 1.4426950408889634
NEG = -1e30
MESH = pl.DeviceIdType.MESH


def attend(
    query_vector,
    own_keys,
    own_values,
    chosen_keys,
    chosen_values,
    key_scale,
    value_scale,
    sel_blocks,
    cutoff,
    positions,
):
    row_count = query_vector.shape[0]
    head_count = query_vector.shape[1]
    head_dim = query_vector.shape[2]
    block_len = own_keys.shape[0]
    all_keys = jnp.concatenate([own_keys, chosen_keys.reshape(-1, head_dim)], axis=0)
    flat_query = query_vector.reshape(row_count * head_count, head_dim)
    scores = lax.dot_general(
        flat_query, all_keys, (((1,), (1,)), ((), ())), preferred_element_type=jnp.float32
    )
    column_scale = jnp.concatenate(
        [jnp.ones((block_len,), jnp.float32), jnp.repeat(key_scale.astype(jnp.float32), block_len)]
    )
    scores = scores * (column_scale / math.sqrt(head_dim))
    scores = scores.reshape(row_count, head_count, -1)
    key_index = jnp.arange(block_len, dtype=jnp.int32)
    own_ok = positions[:, None] >= key_index[None, :]
    sel_ok = (sel_blocks[:, None] * block_len + key_index[None, :] < cutoff).reshape(-1)
    allowed = jnp.concatenate(
        [own_ok, jnp.broadcast_to(sel_ok[None, :], (row_count, sel_ok.shape[0]))], axis=1
    )[:, None, :]
    top_score = jnp.max(jnp.where(allowed, scores, -jnp.inf), axis=-1, keepdims=True)
    weights = jnp.where(allowed, jnp.exp(jnp.where(allowed, scores, top_score) - top_score), 0.0)
    total = jnp.sum(weights, axis=-1, keepdims=True)
    rounded = weights.astype(jnp.bfloat16).reshape(row_count * head_count, -1)
    summed = jnp.dot(rounded[:, :block_len], own_values, preferred_element_type=jnp.float32)
    for index in range(chosen_values.shape[0]):
        piece = rounded[:, (index + 1) * block_len : (index + 2) * block_len]
        summed = summed + value_scale[index].astype(jnp.float32) * jnp.dot(
            piece, chosen_values[index], preferred_element_type=jnp.float32
        )
    return (summed.reshape(row_count, head_count, head_dim) / total).astype(jnp.bfloat16)


def padded(queries, span_keys, span_values, cache_keys, cache_values, start, rows):
    blocks_here = queries.shape[0]
    seq_rank = lax.axis_index("seq")
    wanted = rows[:, 0, 64:70].astype(jnp.int32)
    owner_rank = wanted % NODES
    local_row = wanted // NODES
    is_mine = (owner_rank == seq_rank).astype(jnp.int32)
    ranking = jnp.cumsum(is_mine, axis=1) - 1
    slot_ids = jnp.arange(2, dtype=jnp.int32)
    slot_hits = (is_mine[..., None] == 1) & (ranking[..., None] == slot_ids)
    slot_block = jnp.sum(jnp.where(slot_hits, local_row[..., None], 0), axis=1)
    packed = jnp.concatenate([cache_keys[slot_block, 0], cache_values[slot_block, 0]], axis=-1)
    got_blocks = lax.all_to_all(packed, "seq", split_axis=0, concat_axis=0, tiled=True)
    own_list = wanted[seq_rank]
    own_owner = own_list % NODES
    item_ids = jnp.arange(6, dtype=jnp.int32)
    earlier = (own_owner[:, None] == own_owner[None, :]) & (item_ids[None, :] < item_ids[:, None])
    slot_of = jnp.sum(earlier.astype(jnp.int32), axis=1)
    fetched = got_blocks[own_owner, slot_of].reshape(blocks_here, 3, BLK, 2 * DH)
    row = own_list // NODES
    key_scale = rows[own_owner, 0, row].reshape(blocks_here, 3)
    value_scale = rows[own_owner, 0, ROWS_KV + row].reshape(blocks_here, 3)
    whole = lax.all_to_all(queries, "inter", split_axis=3, concat_axis=2, tiled=True)
    positions = jnp.arange(BLK, dtype=jnp.int32)

    def attend_block(inputs):
        query, keys, values, pack, key_scale, value_scale, ids = inputs
        return attend(
            query, keys, values, pack[..., :DH], pack[..., DH:], key_scale, value_scale, ids, start[0], positions
        )

    result = lax.map(
        attend_block,
        (
            whole.reshape(blocks_here, BLK, HG, DH),
            span_keys[:, 0],
            span_values[:, 0],
            fetched,
            key_scale,
            value_scale,
            own_list.reshape(blocks_here, 3),
        ),
    )
    result = result.reshape(blocks_here, 1, BLK, WIDE)
    return lax.all_to_all(result, "inter", split_axis=2, concat_axis=3, tiled=True)


def path_tables():
    def move(node, way):
        z, x = divmod(node, SIDE)
        dz, dx = ((0, 1), (0, -1), (1, 0), (-1, 0))[way]
        return (z + dz) % SIDE * SIDE + (x + dx) % SIDE

    def paths(here, there):
        if here == there:
            return [[]]
        z, x = divmod(here, SIDE)
        tz, tx = divmod(there, SIDE)
        rx, rz = (tx - x) % SIDE, (tz - z) % SIDE
        ways = [w for w, ok in enumerate((rx in (1, 2), rx in (2, 3), rz in (1, 2), rz in (2, 3))) if ok]
        return [[here * 4 + w] + rest for w in ways for rest in paths(move(here, w), there)]

    table = np.zeros((NODES * NODES, CANDS), np.int32)
    dist = np.zeros((NODES * NODES,), np.int32)
    for owner in range(NODES):
        for dest in range(NODES):
            found = paths(owner, dest)
            pair = owner * NODES + dest
            dist[pair] = len(found[0])
            count = min(CANDS, len(found))
            for c in range(count):
                path = found[c * len(found) // count]
                table[pair, c] = sum(link << (8 * hop) for hop, link in enumerate(path))
    slot_of = np.zeros((256,), np.int32)
    for bit in range(8):
        slot_of[(2 << bit) - 1] = bit
    return np.concatenate([table.reshape(-1), dist, slot_of])


TABLES = path_tables()
DIST_AT = NODES * NODES * CANDS
SLOT_AT = DIST_AT + NODES * NODES
CHOICES = {4: CANDS, 3: CANDS, 2: 2, 1: 1}


def lists_kernel(ks_ref, vs_ref, sel_ref, out_ref, x_ref, buf, send_sem, recv_sem):
    s, r = lax.axis_index("seq"), lax.axis_index("inter")
    barrier = pltpu.get_barrier_semaphore()
    for k in range(1, NODES):
        pl.semaphore_signal(
            barrier, inc=1, device_id=(lax.rem(s + k, NODES), r), device_id_type=MESH
        )
    x_ref[...] = jnp.zeros_like(x_ref)
    x_ref[0:1, 0:ROWS_KV] = ks_ref[...].astype(jnp.float32)
    x_ref[0:1, ROWS_KV : 2 * ROWS_KV] = vs_ref[...].astype(jnp.float32)
    for j in range(2):
        x_ref[0:1, 64 + 3 * j : 67 + 3 * j] = sel_ref[j : j + 1].astype(jnp.float32)
    pl.semaphore_wait(barrier, NODES - 1)
    copies = []
    for k in range(1, NODES):
        copy = pltpu.make_async_remote_copy(
            src_ref=x_ref,
            dst_ref=buf.at[s],
            send_sem=send_sem.at[k],
            recv_sem=recv_sem.at[k],
            device_id=(lax.rem(s + k, NODES), r),
            device_id_type=MESH,
        )
        copy.start()
        copies.append(copy)
    buf[s] = x_ref[...]
    for copy in copies:
        copy.wait()
    out_ref[...] = buf[...]


def plan_kernel(
    rows, start, tab, send, place, limit, factor, flag, occ, bucket, cnt, tbl, posn, front
):
    me = lax.axis_index("seq")

    def clear(ref, count):
        def step(i, _):
            ref[i] = 0
            return 0

        lax.fori_loop(0, count, step, 0, unroll=8)

    clear(front, NODES * 8)
    for t in range(SLOTS):
        for d in range(4):
            tbl[(me * 4 + d) * 8 + t] = 0

    def sort_dest(dest, _):
        for jk in range(6):
            block = rows[dest, 0, 64 + jk].astype(jnp.int32)
            row = block >> 4
            pair = (block & (NODES - 1)) * NODES + dest
            steps = jnp.where(block * BLK < start[0], tab[DIST_AT + pair], 0)
            only = jnp.where(steps == 1, tab[pair * CANDS], NODES * 4)
            occ[only] = occ[only] + LOAD
            item = dest * 8 + jk
            posn[item] = row
            phase = jnp.where(front[item] > 0, 0, 1 + jk // 3)
            kind = jnp.where(steps == 0, 12, phase * 4 + 4 - steps)
            at = cnt[kind]
            bucket[kind * 96 + at] = (pair * CANDS) | (row << 16) | (item << 24)
            cnt[kind] = at + 1
        return 0

    def attempt(carry):
        clear(occ, NODES * 4)
        for kind in range(13):
            cnt[kind] = 0
        lax.fori_loop(0, NODES, sort_dest, 0)

        def run_phase(phase, missed):
            for hops in (4, 3, 2, 1):
                kind = phase * 4 + 4 - hops

                def route(i, missed, kind=kind, hops=hops):
                    entry = bucket[kind * 96 + i]
                    item = entry >> 24
                    row = (entry >> 16) & 255
                    base = entry & 0xFFFF
                    best = None
                    for c in range(CHOICES[hops]):
                        links = tab[base + c]
                        seen, words, ends = 0, 0, 0
                        for h in range(hops):
                            word = occ[(links >> (8 * h)) & 255]
                            used = word | seen
                            seen = used ^ (used + 1)
                            words = words + word
                            ends = ends + (seen << (8 * h))
                        cost = (seen << 16) + words
                        if best is None:
                            best, best_links, best_ends = cost, links, ends
                        else:
                            less = cost < best
                            best = jnp.where(less, cost, best)
                            best_links = jnp.where(less, links, best_links)
                            best_ends = jnp.where(less, ends, best_ends)
                    fits = best < jnp.where((item & 7) < 3, 1 << (16 + SLOTS_FIRST), 1 << (16 + SLOTS))
                    source = row
                    load = LOAD if hops > 1 else 0
                    for h in range(hops):
                        link = (best_links >> (8 * h)) & 255
                        end = (best_ends >> (8 * h)) & 255
                        occ[link] = occ[link] + jnp.where(fits, ((end + 1) >> 1) + load, 0)
                        slot = tab[SLOT_AT + end]
                        tbl[jnp.where(fits, link * 8 + slot, NODES * 4 * 8)] = source
                        source = ROWS_KV + 4 * slot + (link & 3)
                    posn[item] = jnp.where(fits, source, row)
                    late = jnp.where(fits, 0, 1)
                    front[item] = front[item] | late
                    return missed + late

                missed = lax.fori_loop(0, cnt[kind], route, missed)
            return missed

        return lax.fori_loop(0, 3, run_phase, jnp.int32(0)), carry[1] + 1

    missed, _ = lax.while_loop(
        lambda carry: (carry[0] > 0) & (carry[1] < TRIES), attempt, (jnp.int32(1), jnp.int32(0))
    )
    for t in range(SLOTS):
        for d in range(4):
            send[t * 4 + d] = tbl[(me * 4 + d) * 8 + t]
    for jk in range(6):
        block = rows[me, 0, 64 + jk].astype(jnp.int32)
        owner = block & (NODES - 1)
        row = block >> 4
        place[jk] = posn[me * 8 + jk]
        limit[jk] = start[0] - block * BLK
        factor[jk] = rows[owner, 0, row] * (LOG2E / math.sqrt(DH))
        factor[8 + jk] = rows[owner, 0, ROWS_KV + row]
    flag[...] = jnp.full((1, 128), missed, jnp.int32).astype(jnp.float32)


def main_kernel(
    send, place, limit, factor, flag, q, sk_hbm, sv_hbm, ck_hbm, cv_hbm,
    out, over,
    kp, vp, snd, rcv, qb, ob, sk, sv, acc, top, flags,
    load_sem, kv_send, kv_recv, q_send, q_recv, o_send, o_recv, f_send, f_recv,
):
    s, r = lax.axis_index("seq"), lax.axis_index("inter")
    z, x = s // SIDE, s % SIDE
    y, core = r // 2, r % 2
    beside = (
        z * SIDE + (x + 1) % SIDE,
        z * SIDE + (x + 3) % SIDE,
        (z + 1) % SIDE * SIDE + x,
        (z + 3) % SIDE * SIDE + x,
    )

    def peer(k):
        pair = k // 2
        dy = (2 + 3 * pair + 3 * (pair * (pair - 1) // 2)) % 4
        return (y + dy) % 4 * 2 + (core + 1 + k) % 2

    loads = [
        pltpu.make_async_copy(ck_hbm.at[:, 0], kp.at[pl.ds(0, ROWS_KV)], load_sem.at[0]),
        pltpu.make_async_copy(cv_hbm.at[:, 0], vp.at[pl.ds(0, ROWS_KV)], load_sem.at[1]),
        pltpu.make_async_copy(sk_hbm.at[:, 0], sk, load_sem.at[2]),
        pltpu.make_async_copy(sv_hbm.at[:, 0], sv, load_sem.at[3]),
        pltpu.make_async_copy(
            q.at[:, 0, :, pl.ds(pl.multiple_of(r * WIDE, WIDE), WIDE)],
            qb.at[:, pl.ds(pl.multiple_of(r * QROWS, QROWS), QROWS)],
            load_sem.at[4],
        ),
    ]
    for load in loads:
        load.start()

    barrier = pltpu.get_barrier_semaphore()
    for n in beside:
        pl.semaphore_signal(barrier, inc=1, device_id=(n, r), device_id_type=MESH)
    for k in range(PEERS - 1):
        pl.semaphore_signal(barrier, inc=1, device_id=(s, peer(k)), device_id_type=MESH)
    pl.semaphore_wait(barrier, PEERS + 3)

    def kv_copy(t, d, h):
        return pltpu.make_async_remote_copy(
            src_ref=snd.at[t, d, h],
            dst_ref=rcv.at[t, d, h],
            send_sem=kv_send.at[t, d, h],
            recv_sem=kv_recv.at[t, d, h],
            device_id=(beside[d], r),
            device_id_type=MESH,
        )

    def q_copy(k):
        to = peer(k)
        return pltpu.make_async_remote_copy(
            src_ref=q.at[:, 0, :, pl.ds(pl.multiple_of(to * WIDE, WIDE), WIDE)],
            dst_ref=qb.at[:, pl.ds(pl.multiple_of(r * QROWS, QROWS), QROWS)],
            send_sem=q_send.at[k],
            recv_sem=q_recv.at[k],
            device_id=(s, to),
            device_id_type=MESH,
        )

    def f_copy(k):
        return pltpu.make_async_remote_copy(
            src_ref=flag,
            dst_ref=flags.at[r],
            send_sem=f_send.at[k],
            recv_sem=f_recv.at[k],
            device_id=(s, peer(k)),
            device_id_type=MESH,
        )

    def o_copy(j, k):
        to = peer(k)
        return pltpu.make_async_remote_copy(
            src_ref=ob.at[j, pl.ds(pl.multiple_of(to * QROWS, QROWS), QROWS)],
            dst_ref=out.at[j, 0, :, pl.ds(pl.multiple_of(r * WIDE, WIDE), WIDE)],
            send_sem=o_send.at[j, k],
            recv_sem=o_recv.at[j, k],
            device_id=(s, to),
            device_id_type=MESH,
        )

    def o_own(j):
        return pltpu.make_async_copy(
            ob.at[j, pl.ds(pl.multiple_of(r * QROWS, QROWS), QROWS)],
            out.at[j, 0, :, pl.ds(pl.multiple_of(r * WIDE, WIDE), WIDE)],
            load_sem.at[5 + j],
        )

    def pump(t, h):
        pool = (kp, vp)[h]
        if t > 0:
            for d in range(4):
                kv_copy(t - 1, d, h).wait_recv()
            for d in range(4):
                pool[ROWS_KV + 4 * (t - 1) + d] = rcv[t - 1, d, h]
        if t < SLOTS:
            for d in range(4):
                snd[t, d, h] = pool[send[t * 4 + d]]
                kv_copy(t, d, h).start()

    def rows_of(c):
        return pl.ds(pl.multiple_of(c * CROWS, CROWS), CROWS)

    def load_q(j, c):
        tile = qb[j, rows_of(c), :]
        return jnp.concatenate([tile[:, h * DH : (h + 1) * DH] for h in range(HG)], axis=0)

    def scores_of(query, keys):
        return lax.dot_general(
            query, keys, (((1,), (1,)), ((), ())), preferred_element_type=jnp.float32
        )

    ones = jnp.ones((BLK, DH), jnp.bfloat16)
    column = lax.broadcasted_iota(jnp.int32, (1, BLK), 1)

    def own_tile(j, c):
        scores = scores_of(load_q(j, c), sk[j]) * (LOG2E / math.sqrt(DH))
        row = lax.broadcasted_iota(jnp.int32, (TILE_ROWS, 1), 0) % CROWS + c * CROWS
        scores = jnp.where(column <= row, scores, NEG)
        high = jnp.max(scores, axis=1, keepdims=True)
        weights = jnp.exp2(scores - high).astype(jnp.bfloat16)
        acc[j, c] = jnp.dot(
            weights, jnp.concatenate([sv[j], ones], axis=1), preferred_element_type=jnp.float32
        )
        top[j, c] = jnp.broadcast_to(high, (TILE_ROWS, DH))

    def cache_tile(j, c):
        query = load_q(j, c)
        before = top[j, c][:, :1]
        parts = []
        high = before
        for i in range(3 * j, 3 * j + 3):
            bias = jnp.where(column < limit[i], 0.0, NEG)
            part = scores_of(query, kp[place[i]]) * factor[i] + bias
            high = jnp.maximum(high, jnp.max(part, axis=1, keepdims=True))
            parts.append(part)
        fade = jnp.exp2(before - high)
        old = acc[j, c]
        summed = old[:, :DH] * fade
        total = old[:, DH:] * fade
        for i, part in zip(range(3 * j, 3 * j + 3), parts):
            weights = jnp.exp2(part - high).astype(jnp.bfloat16)
            more = jnp.dot(
                weights,
                jnp.concatenate([vp[place[i]], ones], axis=1),
                preferred_element_type=jnp.float32,
            )
            summed = summed + more[:, :DH] * factor[8 + i]
            total = total + more[:, DH:]
        done = (summed / total).astype(jnp.bfloat16)
        for h in range(HG):
            ob[j, rows_of(c), h * DH : (h + 1) * DH] = done[h * CROWS : (h + 1) * CROWS]

    def own_block(j):
        def step(c, _):
            own_tile(j, c)
            return 0

        lax.fori_loop(0, CHIPS, step, 0)

    def cache_blocks(j, begin, end):
        def step(pair, _):
            cache_tile(j, peer(2 * pair) // 2)
            o_copy(j, 2 * pair).start()
            o_copy(j, 2 * pair + 1).start()
            return 0

        lax.fori_loop(begin, min(end, CHIPS - 1), step, 0)
        if end == CHIPS:
            cache_tile(j, y)
            o_copy(j, PEERS - 2).start()
            o_own(j).start()

    for k in range(PEERS - 1):
        q_copy(k).start()
    loads[0].wait()
    pump(0, 0)
    loads[1].wait()
    pump(0, 1)
    for k in range(PEERS - 1):
        f_copy(k).start()
    flags[r] = flag[...]
    for load in loads[2:]:
        load.wait()
    for t in range(1, SLOTS + 1):
        for h in range(2):
            pump(t, h)
            if (t, h) == (3, 0):
                for k in range(PEERS - 1):
                    q_copy(k).wait()
                own_block(0)
            if (t, h) == (4, 0):
                own_block(1)
            if (t, h) == (SLOTS_FIRST, 1):
                cache_blocks(0, 0, 2)
            if (t, h) == (SLOTS_FIRST + 1, 0):
                cache_blocks(0, 2, 3)
            if (t, h) == (SLOTS_FIRST + 1, 1):
                cache_blocks(0, 3, CHIPS)
    cache_blocks(1, 0, CHIPS)
    for k in range(PEERS - 1):
        f_copy(k).wait()
    worst = flags[0]
    for k in range(1, PEERS):
        worst = jnp.maximum(worst, flags[k])
    over[...] = worst
    for t in range(SLOTS):
        for d in range(4):
            for h in range(2):
                kv_copy(t, d, h).wait_send()
    for j in range(2):
        o_own(j).wait()
        for k in range(PEERS - 1):
            o_copy(j, k).wait()


def copy_kernel(x, out, sem):
    copies = [pltpu.make_async_copy(x.at[j], out.at[j], sem.at[j]) for j in range(2)]
    for copy in copies:
        copy.start()
    for copy in copies:
        copy.wait()


def settle(attended):
    hbm = pl.BlockSpec(memory_space=pl.ANY)
    return pl.pallas_call(
        copy_kernel,
        out_shape=jax.ShapeDtypeStruct(attended.shape, attended.dtype),
        in_specs=[hbm],
        out_specs=hbm,
        scratch_shapes=[pltpu.SemaphoreType.DMA((2,))],
        name="settle",
    )(attended)


def per_device(
    queries, span_keys, span_values, cache_keys, cache_values, key_scales, value_scales, selections, start
):
    f32, i32, bf16 = jnp.float32, jnp.int32, jnp.bfloat16
    smem = pl.BlockSpec(memory_space=pltpu.SMEM)
    vmem = pl.BlockSpec(memory_space=pltpu.VMEM)
    hbm = pl.BlockSpec(memory_space=pl.ANY)
    dma = pltpu.SemaphoreType.DMA
    rows = pl.pallas_call(
        lists_kernel,
        out_shape=jax.ShapeDtypeStruct((NODES, 1, 128), f32),
        in_specs=[vmem] * 3,
        out_specs=vmem,
        scratch_shapes=[
            pltpu.VMEM((1, 128), f32),
            pltpu.VMEM((NODES, 1, 128), f32),
            dma((NODES,)),
            dma((NODES,)),
        ],
        compiler_params=pltpu.CompilerParams(collective_id=0, has_side_effects=True),
        name="lists",
    )(key_scales.reshape(1, ROWS_KV), value_scales.reshape(1, ROWS_KV), selections.reshape(2, 3))
    send, place, limit, factor, flag = pl.pallas_call(
        plan_kernel,
        out_shape=(
            jax.ShapeDtypeStruct((4 * SLOTS,), i32),
            jax.ShapeDtypeStruct((8,), i32),
            jax.ShapeDtypeStruct((8,), i32),
            jax.ShapeDtypeStruct((16,), f32),
            jax.ShapeDtypeStruct((1, 128), f32),
        ),
        in_specs=[smem] * 3,
        out_specs=(smem, smem, smem, smem, vmem),
        scratch_shapes=[
            pltpu.SMEM((NODES * 4 + 8,), i32),
            pltpu.SMEM((13 * 96,), i32),
            pltpu.SMEM((16,), i32),
            pltpu.SMEM((NODES * 4 * 8 + 8,), i32),
            pltpu.SMEM((NODES * 8,), i32),
            pltpu.SMEM((NODES * 8,), i32),
        ],
        name="plan",
    )(rows, start, jnp.asarray(TABLES))
    attended, over = pl.pallas_call(
        main_kernel,
        out_shape=(
            jax.ShapeDtypeStruct(queries.shape, bf16),
            jax.ShapeDtypeStruct((1, 128), f32),
        ),
        in_specs=[smem] * 4 + [vmem] + [hbm] * 5,
        out_specs=(hbm, vmem),
        scratch_shapes=[
            pltpu.VMEM((POOL, BLK, DH), bf16),
            pltpu.VMEM((POOL, BLK, DH), bf16),
            pltpu.VMEM((SLOTS, 4, 2, BLK, DH), bf16),
            pltpu.VMEM((SLOTS, 4, 2, BLK, DH), bf16),
            pltpu.VMEM((2, BLK, WIDE), bf16),
            pltpu.VMEM((2, BLK, WIDE), bf16),
            pltpu.VMEM((2, BLK, DH), bf16),
            pltpu.VMEM((2, BLK, DH), bf16),
            pltpu.VMEM((2, CHIPS, TILE_ROWS, 2 * DH), f32),
            pltpu.VMEM((2, CHIPS, TILE_ROWS, DH), f32),
            pltpu.VMEM((PEERS, 1, 128), f32),
            dma((8,)),
            dma((SLOTS, 4, 2)),
            dma((SLOTS, 4, 2)),
            dma((PEERS,)),
            dma((PEERS,)),
            dma((2, PEERS)),
            dma((2, PEERS)),
            dma((PEERS,)),
            dma((PEERS,)),
        ],
        compiler_params=pltpu.CompilerParams(
            collective_id=1, has_side_effects=True, vmem_limit_bytes=56 * 2**20
        ),
        name="exchange_attend",
    )(send, place, limit, factor, flag, queries, span_keys, span_values, cache_keys, cache_values)
    return lax.cond(
        over[0, 0] > 0,
        lambda: padded(queries, span_keys, span_values, cache_keys, cache_values, start, rows),
        lambda: settle(attended),
    )


def solution(mesh):
    placed = (
        P(None, "seq", "inter", None),
        P(None, "seq", None, "inter"),
        P(None, "seq", None, "inter"),
        P(None, "seq", None, "inter"),
        P(None, "seq", None, "inter"),
        P(None, "seq", "inter"),
        P(None, "seq", "inter"),
        P(None, "seq", "inter", None),
        P(),
    )
    return jax.shard_map(
        per_device,
        mesh=mesh,
        in_specs=placed,
        out_specs=P(None, "seq", "inter", None),
        check_vma=False,
    )
```

```python
import functools
import math

import jax
import jax.numpy as jnp
import numpy as np
from jax import lax
from jax.experimental import pallas as pl
from jax.experimental.pallas import tpu as pltpu
from jax.sharding import PartitionSpec as P

DH = 128
BLK = 512
HG = 4
SIDE = 4
NODES = SIDE * SIDE
ROWS_KV = 32
SLOTS = 6
SLOTS_FIRST = 4
CANDS = 6
TRIES = 10
LOAD = 256
PEERS = 8
QROWS = BLK // PEERS
WIDE = HG * DH
TILE_ROWS = HG * QROWS
POOL = ROWS_KV + 4 * SLOTS
LOG2E = 1.4426950408889634
NEG = -1e30
MESH = pl.DeviceIdType.MESH


def attend(
    query_vector,
    own_keys,
    own_values,
    chosen_keys,
    chosen_values,
    key_scale,
    value_scale,
    sel_blocks,
    cutoff,
    positions,
):
    row_count = query_vector.shape[0]
    head_count = query_vector.shape[1]
    head_dim = query_vector.shape[2]
    block_len = own_keys.shape[0]
    all_keys = jnp.concatenate([own_keys, chosen_keys.reshape(-1, head_dim)], axis=0)
    flat_query = query_vector.reshape(row_count * head_count, head_dim)
    scores = lax.dot_general(
        flat_query, all_keys, (((1,), (1,)), ((), ())), preferred_element_type=jnp.float32
    )
    column_scale = jnp.concatenate(
        [jnp.ones((block_len,), jnp.float32), jnp.repeat(key_scale.astype(jnp.float32), block_len)]
    )
    scores = scores * (column_scale / math.sqrt(head_dim))
    scores = scores.reshape(row_count, head_count, -1)
    key_index = jnp.arange(block_len, dtype=jnp.int32)
    own_ok = positions[:, None] >= key_index[None, :]
    sel_ok = (sel_blocks[:, None] * block_len + key_index[None, :] < cutoff).reshape(-1)
    allowed = jnp.concatenate(
        [own_ok, jnp.broadcast_to(sel_ok[None, :], (row_count, sel_ok.shape[0]))], axis=1
    )[:, None, :]
    top_score = jnp.max(jnp.where(allowed, scores, -jnp.inf), axis=-1, keepdims=True)
    weights = jnp.where(allowed, jnp.exp(jnp.where(allowed, scores, top_score) - top_score), 0.0)
    total = jnp.sum(weights, axis=-1, keepdims=True)
    rounded = weights.astype(jnp.bfloat16).reshape(row_count * head_count, -1)
    summed = jnp.dot(rounded[:, :block_len], own_values, preferred_element_type=jnp.float32)
    for index in range(chosen_values.shape[0]):
        piece = rounded[:, (index + 1) * block_len : (index + 2) * block_len]
        summed = summed + value_scale[index].astype(jnp.float32) * jnp.dot(
            piece, chosen_values[index], preferred_element_type=jnp.float32
        )
    return (summed.reshape(row_count, head_count, head_dim) / total).astype(jnp.bfloat16)


def padded(queries, span_keys, span_values, cache_keys, cache_values, start, rows):
    blocks_here = queries.shape[0]
    seq_rank = lax.axis_index("seq")
    wanted = rows[:, 0, 64:70].astype(jnp.int32)
    owner_rank = wanted % NODES
    local_row = wanted // NODES
    is_mine = (owner_rank == seq_rank).astype(jnp.int32)
    ranking = jnp.cumsum(is_mine, axis=1) - 1
    slot_ids = jnp.arange(2, dtype=jnp.int32)
    slot_hits = (is_mine[..., None] == 1) & (ranking[..., None] == slot_ids)
    slot_block = jnp.sum(jnp.where(slot_hits, local_row[..., None], 0), axis=1)
    packed = jnp.concatenate([cache_keys[slot_block, 0], cache_values[slot_block, 0]], axis=-1)
    got_blocks = lax.all_to_all(packed, "seq", split_axis=0, concat_axis=0, tiled=True)
    own_list = wanted[seq_rank]
    own_owner = own_list % NODES
    item_ids = jnp.arange(6, dtype=jnp.int32)
    earlier = (own_owner[:, None] == own_owner[None, :]) & (item_ids[None, :] < item_ids[:, None])
    slot_of = jnp.sum(earlier.astype(jnp.int32), axis=1)
    fetched = got_blocks[own_owner, slot_of].reshape(blocks_here, 3, BLK, 2 * DH)
    row = own_list // NODES
    key_scale = rows[own_owner, 0, row].reshape(blocks_here, 3)
    value_scale = rows[own_owner, 0, ROWS_KV + row].reshape(blocks_here, 3)
    whole = lax.all_to_all(queries, "inter", split_axis=3, concat_axis=2, tiled=True)
    positions = jnp.arange(BLK, dtype=jnp.int32)

    def attend_block(inputs):
        query, keys, values, pack, key_scale, value_scale, ids = inputs
        return attend(
            query, keys, values, pack[..., :DH], pack[..., DH:], key_scale, value_scale, ids, start[0], positions
        )

    result = lax.map(
        attend_block,
        (
            whole.reshape(blocks_here, BLK, HG, DH),
            span_keys[:, 0],
            span_values[:, 0],
            fetched,
            key_scale,
            value_scale,
            own_list.reshape(blocks_here, 3),
        ),
    )
    result = result.reshape(blocks_here, 1, BLK, WIDE)
    return lax.all_to_all(result, "inter", split_axis=2, concat_axis=3, tiled=True)


def path_tables():
    def move(node, way):
        z, x = divmod(node, SIDE)
        dz, dx = ((0, 1), (0, -1), (1, 0), (-1, 0))[way]
        return (z + dz) % SIDE * SIDE + (x + dx) % SIDE

    def paths(here, there):
        if here == there:
            return [[]]
        z, x = divmod(here, SIDE)
        tz, tx = divmod(there, SIDE)
        rx, rz = (tx - x) % SIDE, (tz - z) % SIDE
        ways = [w for w, ok in enumerate((rx in (1, 2), rx in (2, 3), rz in (1, 2), rz in (2, 3))) if ok]
        return [[here * 4 + w] + rest for w in ways for rest in paths(move(here, w), there)]

    table = np.zeros((NODES * NODES, CANDS), np.int32)
    dist = np.zeros((NODES * NODES,), np.int32)
    for owner in range(NODES):
        for dest in range(NODES):
            found = paths(owner, dest)
            pair = owner * NODES + dest
            dist[pair] = len(found[0])
            count = min(CANDS, len(found))
            for c in range(count):
                path = found[c * len(found) // count]
                table[pair, c] = sum(link << (8 * hop) for hop, link in enumerate(path))
    slot_of = np.zeros((256,), np.int32)
    for bit in range(8):
        slot_of[(2 << bit) - 1] = bit
    return np.concatenate([table.reshape(-1), dist, slot_of])


TABLES = path_tables()
DIST_AT = NODES * NODES * CANDS
SLOT_AT = DIST_AT + NODES * NODES
CHOICES = {4: CANDS, 3: CANDS, 2: 2, 1: 1}


def lists_kernel(ks_ref, vs_ref, sel_ref, out_ref, x_ref, buf, send_sem, recv_sem):
    s, r = lax.axis_index("seq"), lax.axis_index("inter")
    barrier = pltpu.get_barrier_semaphore()
    for k in range(1, NODES):
        pl.semaphore_signal(
            barrier, inc=1, device_id=(lax.rem(s + k, NODES), r), device_id_type=MESH
        )
    x_ref[...] = jnp.zeros_like(x_ref)
    x_ref[0:1, 0:ROWS_KV] = ks_ref[...].astype(jnp.float32)
    x_ref[0:1, ROWS_KV : 2 * ROWS_KV] = vs_ref[...].astype(jnp.float32)
    for j in range(2):
        x_ref[0:1, 64 + 3 * j : 67 + 3 * j] = sel_ref[j : j + 1].astype(jnp.float32)
    pl.semaphore_wait(barrier, NODES - 1)
    copies = []
    for k in range(1, NODES):
        copy = pltpu.make_async_remote_copy(
            src_ref=x_ref,
            dst_ref=buf.at[s],
            send_sem=send_sem.at[k],
            recv_sem=recv_sem.at[k],
            device_id=(lax.rem(s + k, NODES), r),
            device_id_type=MESH,
        )
        copy.start()
        copies.append(copy)
    buf[s] = x_ref[...]
    for copy in copies:
        copy.wait()
    out_ref[...] = buf[...]


def plan_kernel(
    rows, start, tab, send, place, limit, factor, flag, occ, bucket, cnt, tbl, posn, front
):
    me = lax.axis_index("seq")

    def clear(ref, count):
        def step(i, _):
            ref[i] = 0
            return 0

        lax.fori_loop(0, count, step, 0, unroll=8)

    clear(front, NODES * 8)
    for t in range(SLOTS):
        for d in range(4):
            tbl[(me * 4 + d) * 8 + t] = 0

    def sort_dest(dest, _):
        for jk in range(6):
            block = rows[dest, 0, 64 + jk].astype(jnp.int32)
            row = block >> 4
            pair = (block & (NODES - 1)) * NODES + dest
            steps = jnp.where(block * BLK < start[0], tab[DIST_AT + pair], 0)
            only = jnp.where(steps == 1, tab[pair * CANDS], NODES * 4)
            occ[only] = occ[only] + LOAD
            item = dest * 8 + jk
            posn[item] = row
            phase = jnp.where(front[item] > 0, 0, 1 + jk // 3)
            kind = jnp.where(steps == 0, 12, phase * 4 + 4 - steps)
            at = cnt[kind]
            bucket[kind * 96 + at] = (pair * CANDS) | (row << 16) | (item << 24)
            cnt[kind] = at + 1
        return 0

    def attempt(carry):
        clear(occ, NODES * 4)
        for kind in range(13):
            cnt[kind] = 0
        lax.fori_loop(0, NODES, sort_dest, 0)
        for kind in range(12):
            bucket[kind * 96 + cnt[kind]] = 0

        def run_phase(phase, missed):
            for hops in (4, 3, 2, 1):
                kind = phase * 4 + 4 - hops

                def fetch(i, kind=kind, hops=hops):
                    entry = bucket[kind * 96 + i]
                    return (entry,) + tuple(tab[(entry & 0xFFFF) + c] for c in range(CHOICES[hops]))

                def route(i, carry, hops=hops, fetch=fetch):
                    missed, entry = carry[:2]
                    upcoming = fetch(i + 1)
                    item = entry >> 24
                    row = (entry >> 16) & 255
                    best = None
                    for links in carry[2:]:
                        seen, words, ends = 0, 0, 0
                        for h in range(hops):
                            word = occ[(links >> (8 * h)) & 255]
                            used = word | seen
                            seen = used ^ (used + 1)
                            words = words + word
                            ends = ends + (seen << (8 * h))
                        cost = (seen << 16) + words
                        if best is None:
                            best, best_links, best_ends = cost, links, ends
                        else:
                            less = cost < best
                            best = jnp.where(less, cost, best)
                            best_links = jnp.where(less, links, best_links)
                            best_ends = jnp.where(less, ends, best_ends)
                    fits = best < jnp.where((item & 7) < 3, 1 << (16 + SLOTS_FIRST), 1 << (16 + SLOTS))
                    source = row
                    load = LOAD if hops > 1 else 0
                    for h in range(hops):
                        link = (best_links >> (8 * h)) & 255
                        end = (best_ends >> (8 * h)) & 255
                        occ[link] = occ[link] + jnp.where(fits, ((end + 1) >> 1) + load, 0)
                        slot = tab[SLOT_AT + end]
                        tbl[jnp.where(fits, link * 8 + slot, NODES * 4 * 8)] = source
                        source = ROWS_KV + 4 * slot + (link & 3)
                    posn[item] = jnp.where(fits, source, row)
                    late = jnp.where(fits, 0, 1)
                    front[item] = front[item] | late
                    return (missed + late,) + upcoming

                missed = lax.fori_loop(0, cnt[kind], route, (missed,) + fetch(0))[0]
            return missed

        return lax.fori_loop(0, 3, run_phase, jnp.int32(0)), carry[1] + 1

    missed, _ = lax.while_loop(
        lambda carry: (carry[0] > 0) & (carry[1] < TRIES), attempt, (jnp.int32(1), jnp.int32(0))
    )
    for t in range(SLOTS):
        for d in range(4):
            send[t * 4 + d] = tbl[(me * 4 + d) * 8 + t]
    for jk in range(6):
        block = rows[me, 0, 64 + jk].astype(jnp.int32)
        owner = block & (NODES - 1)
        row = block >> 4
        place[jk] = posn[me * 8 + jk]
        limit[jk] = start[0] - block * BLK
        factor[jk] = rows[owner, 0, row] * (LOG2E / math.sqrt(DH))
        factor[8 + jk] = rows[owner, 0, ROWS_KV + row]
    flag[...] = jnp.full((1, 128), missed, jnp.int32).astype(jnp.float32)


def main_kernel(
    send, place, limit, factor, flag, q, sk_hbm, sv_hbm, ck_hbm, cv_hbm,
    out, over,
    kp, vp, snd, rcv, qb, ob, sk, sv, acc, top, even, odd, even_top, odd_top, flags,
    load_sem, kv_send, kv_recv, q_send, q_recv, o_send, o_recv, f_send, f_recv,
):
    s, r = lax.axis_index("seq"), lax.axis_index("inter")
    z, x = s // SIDE, s % SIDE
    y, core = r // 2, r % 2
    beside = (
        z * SIDE + (x + 1) % SIDE,
        z * SIDE + (x + 3) % SIDE,
        (z + 1) % SIDE * SIDE + x,
        (z + 3) % SIDE * SIDE + x,
    )

    def peer(k):
        pair = k // 2
        dy = (2 + 3 * pair + 3 * (pair * (pair - 1) // 2)) % 4
        return (y + dy) % 4 * 2 + (core + 1 + k) % 2

    loads = [
        pltpu.make_async_copy(ck_hbm.at[:, 0], kp.at[pl.ds(0, ROWS_KV)], load_sem.at[0]),
        pltpu.make_async_copy(cv_hbm.at[:, 0], vp.at[pl.ds(0, ROWS_KV)], load_sem.at[1]),
        pltpu.make_async_copy(sk_hbm.at[:, 0], sk, load_sem.at[2]),
        pltpu.make_async_copy(sv_hbm.at[:, 0], sv, load_sem.at[3]),
        pltpu.make_async_copy(
            q.at[:, 0, :, pl.ds(pl.multiple_of(r * WIDE, WIDE), WIDE)],
            qb.at[:, pl.ds(pl.multiple_of(r * QROWS, QROWS), QROWS)],
            load_sem.at[4],
        ),
    ]
    for load in loads:
        load.start()

    barrier = pltpu.get_barrier_semaphore()
    for n in beside:
        pl.semaphore_signal(barrier, inc=1, device_id=(n, r), device_id_type=MESH)
    for k in range(PEERS - 1):
        pl.semaphore_signal(barrier, inc=1, device_id=(s, peer(k)), device_id_type=MESH)
    pl.semaphore_wait(barrier, PEERS + 3)

    def kv_copy(t, d, h):
        return pltpu.make_async_remote_copy(
            src_ref=snd.at[t, d, h],
            dst_ref=rcv.at[t, d, h],
            send_sem=kv_send.at[t, d, h],
            recv_sem=kv_recv.at[t, d, h],
            device_id=(beside[d], r),
            device_id_type=MESH,
        )

    def q_copy(k):
        to = peer(k)
        return pltpu.make_async_remote_copy(
            src_ref=q.at[:, 0, :, pl.ds(pl.multiple_of(to * WIDE, WIDE), WIDE)],
            dst_ref=qb.at[:, pl.ds(pl.multiple_of(r * QROWS, QROWS), QROWS)],
            send_sem=q_send.at[k],
            recv_sem=q_recv.at[k],
            device_id=(s, to),
            device_id_type=MESH,
        )

    def f_copy(k):
        return pltpu.make_async_remote_copy(
            src_ref=flag,
            dst_ref=flags.at[r],
            send_sem=f_send.at[k],
            recv_sem=f_recv.at[k],
            device_id=(s, peer(k)),
            device_id_type=MESH,
        )

    def o_copy(j, k):
        to = peer(k)
        return pltpu.make_async_remote_copy(
            src_ref=ob.at[j, pl.ds(pl.multiple_of(to * QROWS, QROWS), QROWS)],
            dst_ref=out.at[j, 0, :, pl.ds(pl.multiple_of(r * WIDE, WIDE), WIDE)],
            send_sem=o_send.at[j, k],
            recv_sem=o_recv.at[j, k],
            device_id=(s, to),
            device_id_type=MESH,
        )

    def o_own(j):
        return pltpu.make_async_copy(
            ob.at[j, pl.ds(pl.multiple_of(r * QROWS, QROWS), QROWS)],
            out.at[j, 0, :, pl.ds(pl.multiple_of(r * WIDE, WIDE), WIDE)],
            load_sem.at[5 + j],
        )

    def pump(t, h):
        pool = (kp, vp)[h]
        if t > 0:
            for d in range(4):
                kv_copy(t - 1, d, h).wait_recv()
            for d in range(4):
                pool[ROWS_KV + 4 * (t - 1) + d] = rcv[t - 1, d, h]
        if t < SLOTS:
            for d in range(4):
                snd[t, d, h] = pool[send[t * 4 + d]]
                kv_copy(t, d, h).start()

    def rows_of(c):
        return pl.ds(pl.multiple_of(c * QROWS, QROWS), QROWS)

    def load_q(j, c):
        tile = qb[j, rows_of(c), :]
        return jnp.concatenate([tile[:, h * DH : (h + 1) * DH] for h in range(HG)], axis=0)

    def scores_of(query, keys):
        return lax.dot_general(
            query, keys, (((1,), (1,)), ((), ())), preferred_element_type=jnp.float32
        )

    ones = jnp.ones((BLK, DH), jnp.bfloat16)
    column = lax.broadcasted_iota(jnp.int32, (1, BLK), 1)

    def own_tile(j, c):
        scores = scores_of(load_q(j, c), sk[j]) * (LOG2E / math.sqrt(DH))
        row = lax.broadcasted_iota(jnp.int32, (TILE_ROWS, 1), 0) % QROWS + c * QROWS
        scores = jnp.where(column <= row, scores, NEG)
        high = jnp.max(scores, axis=1, keepdims=True)
        weights = jnp.exp2(scores - high).astype(jnp.bfloat16)
        acc[j, c] = jnp.dot(
            weights, jnp.concatenate([sv[j], ones], axis=1), preferred_element_type=jnp.float32
        )
        top[j, c] = jnp.broadcast_to(high, (TILE_ROWS, DH))

    def score(j, k, held, held_top):
        c = peer(k)
        query = load_q(j, c)
        high = top[j, c][:, :1]
        for i in range(3):
            bias = jnp.where(column < limit[3 * j + i], 0.0, NEG)
            part = scores_of(query, kp[place[3 * j + i]]) * factor[3 * j + i] + bias
            high = jnp.maximum(high, jnp.max(part, axis=1, keepdims=True))
            held[i] = part
        held_top[...] = jnp.broadcast_to(high, (TILE_ROWS, DH))

    def attend_tile(j, k, held, held_top):
        c = peer(k)
        high = held_top[...]
        fade = jnp.exp2(top[j, c] - high)
        old = acc[j, c]
        summed = old[:, :DH] * fade
        total = old[:, DH:] * fade
        for i in range(3):
            weights = jnp.exp2(held[i] - high[:, :1]).astype(jnp.bfloat16)
            more = jnp.dot(
                weights,
                jnp.concatenate([vp[place[3 * j + i]], ones], axis=1),
                preferred_element_type=jnp.float32,
            )
            summed = summed + more[:, :DH] * factor[8 + 3 * j + i]
            total = total + more[:, DH:]
        done = (summed / total).astype(jnp.bfloat16)
        for h in range(HG):
            ob[j, rows_of(c), h * DH : (h + 1) * DH] = done[h * QROWS : (h + 1) * QROWS]

    def own_block(j):
        def step(c, _):
            own_tile(j, c)
            return 0

        lax.fori_loop(0, PEERS, step, 0)

    def cache_blocks(j, begin, end):
        def step(pair, _):
            score(j, 2 * pair + 1, odd, odd_top)
            attend_tile(j, 2 * pair, even, even_top)
            o_copy(j, 2 * pair).start()
            score(j, 2 * pair + 2, even, even_top)
            attend_tile(j, 2 * pair + 1, odd, odd_top)
            o_copy(j, 2 * pair + 1).start()
            return 0

        if begin == 0:
            score(j, 0, even, even_top)
        lax.fori_loop(begin // 2, min(end, PEERS - 2) // 2, step, 0)
        if end == PEERS:
            score(j, PEERS - 1, odd, odd_top)
            attend_tile(j, PEERS - 2, even, even_top)
            o_copy(j, PEERS - 2).start()
            attend_tile(j, PEERS - 1, odd, odd_top)
            o_own(j).start()

    for k in range(PEERS - 1):
        q_copy(k).start()
    loads[0].wait()
    pump(0, 0)
    loads[1].wait()
    pump(0, 1)
    for k in range(PEERS - 1):
        f_copy(k).start()
    flags[r] = flag[...]
    for load in loads[2:]:
        load.wait()
    for t in range(1, SLOTS + 1):
        for h in range(2):
            pump(t, h)
            if (t, h) == (3, 0):
                for k in range(PEERS - 1):
                    q_copy(k).wait()
                own_block(0)
            if (t, h) == (4, 0):
                own_block(1)
            if (t, h) == (SLOTS_FIRST, 1):
                cache_blocks(0, 0, 2)
            if (t, h) == (SLOTS_FIRST + 1, 0):
                cache_blocks(0, 2, 4)
            if (t, h) == (SLOTS_FIRST + 1, 1):
                cache_blocks(0, 4, PEERS)
    cache_blocks(1, 0, PEERS)
    for k in range(PEERS - 1):
        f_copy(k).wait()
    worst = flags[0]
    for k in range(1, PEERS):
        worst = jnp.maximum(worst, flags[k])
    over[...] = worst
    for t in range(SLOTS):
        for d in range(4):
            for h in range(2):
                kv_copy(t, d, h).wait_send()
    for j in range(2):
        o_own(j).wait()
        for k in range(PEERS - 1):
            o_copy(j, k).wait()


def copy_kernel(x, out, sem):
    copies = [pltpu.make_async_copy(x.at[j], out.at[j], sem.at[j]) for j in range(2)]
    for copy in copies:
        copy.start()
    for copy in copies:
        copy.wait()


def settle(attended):
    hbm = pl.BlockSpec(memory_space=pl.ANY)
    return pl.pallas_call(
        copy_kernel,
        out_shape=jax.ShapeDtypeStruct(attended.shape, attended.dtype),
        in_specs=[hbm],
        out_specs=hbm,
        scratch_shapes=[pltpu.SemaphoreType.DMA((2,))],
        name="settle",
    )(attended)


def per_device(
    queries, span_keys, span_values, cache_keys, cache_values, key_scales, value_scales, selections, start
):
    f32, i32, bf16 = jnp.float32, jnp.int32, jnp.bfloat16
    smem = pl.BlockSpec(memory_space=pltpu.SMEM)
    vmem = pl.BlockSpec(memory_space=pltpu.VMEM)
    hbm = pl.BlockSpec(memory_space=pl.ANY)
    dma = pltpu.SemaphoreType.DMA
    rows = pl.pallas_call(
        lists_kernel,
        out_shape=jax.ShapeDtypeStruct((NODES, 1, 128), f32),
        in_specs=[vmem] * 3,
        out_specs=vmem,
        scratch_shapes=[
            pltpu.VMEM((1, 128), f32),
            pltpu.VMEM((NODES, 1, 128), f32),
            dma((NODES,)),
            dma((NODES,)),
        ],
        compiler_params=pltpu.CompilerParams(collective_id=0, has_side_effects=True),
        name="lists",
    )(key_scales.reshape(1, ROWS_KV), value_scales.reshape(1, ROWS_KV), selections.reshape(2, 3))
    send, place, limit, factor, flag = pl.pallas_call(
        plan_kernel,
        out_shape=(
            jax.ShapeDtypeStruct((4 * SLOTS,), i32),
            jax.ShapeDtypeStruct((8,), i32),
            jax.ShapeDtypeStruct((8,), i32),
            jax.ShapeDtypeStruct((16,), f32),
            jax.ShapeDtypeStruct((1, 128), f32),
        ),
        in_specs=[smem] * 3,
        out_specs=(smem, smem, smem, smem, vmem),
        scratch_shapes=[
            pltpu.SMEM((NODES * 4 + 8,), i32),
            pltpu.SMEM((13 * 96 + 8,), i32),
            pltpu.SMEM((16,), i32),
            pltpu.SMEM((NODES * 4 * 8 + 8,), i32),
            pltpu.SMEM((NODES * 8,), i32),
            pltpu.SMEM((NODES * 8,), i32),
        ],
        name="plan",
    )(rows, start, jnp.asarray(TABLES))
    attended, over = pl.pallas_call(
        main_kernel,
        out_shape=(
            jax.ShapeDtypeStruct(queries.shape, bf16),
            jax.ShapeDtypeStruct((1, 128), f32),
        ),
        in_specs=[smem] * 4 + [vmem] + [hbm] * 5,
        out_specs=(hbm, vmem),
        scratch_shapes=[
            pltpu.VMEM((POOL, BLK, DH), bf16),
            pltpu.VMEM((POOL, BLK, DH), bf16),
            pltpu.VMEM((SLOTS, 4, 2, BLK, DH), bf16),
            pltpu.VMEM((SLOTS, 4, 2, BLK, DH), bf16),
            pltpu.VMEM((2, BLK, WIDE), bf16),
            pltpu.VMEM((2, BLK, WIDE), bf16),
            pltpu.VMEM((2, BLK, DH), bf16),
            pltpu.VMEM((2, BLK, DH), bf16),
            pltpu.VMEM((2, PEERS, TILE_ROWS, 2 * DH), f32),
            pltpu.VMEM((2, PEERS, TILE_ROWS, DH), f32),
            pltpu.VMEM((3, TILE_ROWS, BLK), f32),
            pltpu.VMEM((3, TILE_ROWS, BLK), f32),
            pltpu.VMEM((TILE_ROWS, DH), f32),
            pltpu.VMEM((TILE_ROWS, DH), f32),
            pltpu.VMEM((PEERS, 1, 128), f32),
            dma((8,)),
            dma((SLOTS, 4, 2)),
            dma((SLOTS, 4, 2)),
            dma((PEERS,)),
            dma((PEERS,)),
            dma((2, PEERS)),
            dma((2, PEERS)),
            dma((PEERS,)),
            dma((PEERS,)),
        ],
        compiler_params=pltpu.CompilerParams(
            collective_id=1, has_side_effects=True, vmem_limit_bytes=56 * 2**20
        ),
        name="exchange_attend",
    )(send, place, limit, factor, flag, queries, span_keys, span_values, cache_keys, cache_values)
    return lax.cond(
        over[0, 0] > 0,
        lambda: padded(queries, span_keys, span_values, cache_keys, cache_values, start, rows),
        lambda: settle(attended),
    )


def solution(mesh):
    placed = (
        P(None, "seq", "inter", None),
        P(None, "seq", None, "inter"),
        P(None, "seq", None, "inter"),
        P(None, "seq", None, "inter"),
        P(None, "seq", None, "inter"),
        P(None, "seq", "inter"),
        P(None, "seq", "inter"),
        P(None, "seq", "inter", None),
        P(),
    )
    return jax.shard_map(
        per_device,
        mesh=mesh,
        in_specs=placed,
        out_specs=P(None, "seq", "inter", None),
        check_vma=False,
    )
```

```python
import functools
import math

import jax
import jax.numpy as jnp
import numpy as np
from jax import lax
from jax.experimental import pallas as pl
from jax.experimental.pallas import tpu as pltpu
from jax.sharding import PartitionSpec as P

DH = 128
BLK = 512
HG = 4
SIDE = 4
NODES = SIDE * SIDE
ROWS_KV = 32
SLOTS = 6
SLOTS_FIRST = 4
CANDS = 6
TRIES = 10
LOAD = 256
PEERS = 8
QROWS = BLK // PEERS
WIDE = HG * DH
TILE_ROWS = HG * QROWS
POOL = ROWS_KV + 4 * SLOTS
LOG2E = 1.4426950408889634
NEG = -1e30
MESH = pl.DeviceIdType.MESH


def attend(
    query_vector,
    own_keys,
    own_values,
    chosen_keys,
    chosen_values,
    key_scale,
    value_scale,
    sel_blocks,
    cutoff,
    positions,
):
    row_count = query_vector.shape[0]
    head_count = query_vector.shape[1]
    head_dim = query_vector.shape[2]
    block_len = own_keys.shape[0]
    all_keys = jnp.concatenate([own_keys, chosen_keys.reshape(-1, head_dim)], axis=0)
    flat_query = query_vector.reshape(row_count * head_count, head_dim)
    scores = lax.dot_general(
        flat_query, all_keys, (((1,), (1,)), ((), ())), preferred_element_type=jnp.float32
    )
    column_scale = jnp.concatenate(
        [jnp.ones((block_len,), jnp.float32), jnp.repeat(key_scale.astype(jnp.float32), block_len)]
    )
    scores = scores * (column_scale / math.sqrt(head_dim))
    scores = scores.reshape(row_count, head_count, -1)
    key_index = jnp.arange(block_len, dtype=jnp.int32)
    own_ok = positions[:, None] >= key_index[None, :]
    sel_ok = (sel_blocks[:, None] * block_len + key_index[None, :] < cutoff).reshape(-1)
    allowed = jnp.concatenate(
        [own_ok, jnp.broadcast_to(sel_ok[None, :], (row_count, sel_ok.shape[0]))], axis=1
    )[:, None, :]
    top_score = jnp.max(jnp.where(allowed, scores, -jnp.inf), axis=-1, keepdims=True)
    weights = jnp.where(allowed, jnp.exp(jnp.where(allowed, scores, top_score) - top_score), 0.0)
    total = jnp.sum(weights, axis=-1, keepdims=True)
    rounded = weights.astype(jnp.bfloat16).reshape(row_count * head_count, -1)
    summed = jnp.dot(rounded[:, :block_len], own_values, preferred_element_type=jnp.float32)
    for index in range(chosen_values.shape[0]):
        piece = rounded[:, (index + 1) * block_len : (index + 2) * block_len]
        summed = summed + value_scale[index].astype(jnp.float32) * jnp.dot(
            piece, chosen_values[index], preferred_element_type=jnp.float32
        )
    return (summed.reshape(row_count, head_count, head_dim) / total).astype(jnp.bfloat16)


def padded(queries, span_keys, span_values, cache_keys, cache_values, start, rows):
    blocks_here = queries.shape[0]
    seq_rank = lax.axis_index("seq")
    wanted = rows[:, 0, 64:70].astype(jnp.int32)
    owner_rank = wanted % NODES
    local_row = wanted // NODES
    is_mine = (owner_rank == seq_rank).astype(jnp.int32)
    ranking = jnp.cumsum(is_mine, axis=1) - 1
    slot_ids = jnp.arange(2, dtype=jnp.int32)
    slot_hits = (is_mine[..., None] == 1) & (ranking[..., None] == slot_ids)
    slot_block = jnp.sum(jnp.where(slot_hits, local_row[..., None], 0), axis=1)
    packed = jnp.concatenate([cache_keys[slot_block, 0], cache_values[slot_block, 0]], axis=-1)
    got_blocks = lax.all_to_all(packed, "seq", split_axis=0, concat_axis=0, tiled=True)
    own_list = wanted[seq_rank]
    own_owner = own_list % NODES
    item_ids = jnp.arange(6, dtype=jnp.int32)
    earlier = (own_owner[:, None] == own_owner[None, :]) & (item_ids[None, :] < item_ids[:, None])
    slot_of = jnp.sum(earlier.astype(jnp.int32), axis=1)
    fetched = got_blocks[own_owner, slot_of].reshape(blocks_here, 3, BLK, 2 * DH)
    row = own_list // NODES
    key_scale = rows[own_owner, 0, row].reshape(blocks_here, 3)
    value_scale = rows[own_owner, 0, ROWS_KV + row].reshape(blocks_here, 3)
    whole = lax.all_to_all(queries, "inter", split_axis=3, concat_axis=2, tiled=True)
    positions = jnp.arange(BLK, dtype=jnp.int32)

    def attend_block(inputs):
        query, keys, values, pack, key_scale, value_scale, ids = inputs
        return attend(
            query, keys, values, pack[..., :DH], pack[..., DH:], key_scale, value_scale, ids, start[0], positions
        )

    result = lax.map(
        attend_block,
        (
            whole.reshape(blocks_here, BLK, HG, DH),
            span_keys[:, 0],
            span_values[:, 0],
            fetched,
            key_scale,
            value_scale,
            own_list.reshape(blocks_here, 3),
        ),
    )
    result = result.reshape(blocks_here, 1, BLK, WIDE)
    return lax.all_to_all(result, "inter", split_axis=2, concat_axis=3, tiled=True)


def path_tables():
    def move(node, way):
        z, x = divmod(node, SIDE)
        dz, dx = ((0, 1), (0, -1), (1, 0), (-1, 0))[way]
        return (z + dz) % SIDE * SIDE + (x + dx) % SIDE

    def paths(here, there):
        if here == there:
            return [[]]
        z, x = divmod(here, SIDE)
        tz, tx = divmod(there, SIDE)
        rx, rz = (tx - x) % SIDE, (tz - z) % SIDE
        ways = [w for w, ok in enumerate((rx in (1, 2), rx in (2, 3), rz in (1, 2), rz in (2, 3))) if ok]
        return [[here * 4 + w] + rest for w in ways for rest in paths(move(here, w), there)]

    table = np.zeros((NODES * NODES, CANDS), np.int32)
    dist = np.zeros((NODES * NODES,), np.int32)
    for owner in range(NODES):
        for dest in range(NODES):
            found = paths(owner, dest)
            pair = owner * NODES + dest
            dist[pair] = len(found[0])
            count = min(CANDS, len(found))
            for c in range(count):
                path = found[c * len(found) // count]
                table[pair, c] = sum(link << (8 * hop) for hop, link in enumerate(path))
    slot_of = np.zeros((256,), np.int32)
    for bit in range(8):
        slot_of[(2 << bit) - 1] = bit
    return np.concatenate([table.reshape(-1), dist, slot_of])


TABLES = path_tables()
DIST_AT = NODES * NODES * CANDS
SLOT_AT = DIST_AT + NODES * NODES
CHOICES = {4: CANDS, 3: CANDS, 2: 2, 1: 1}


def lists_kernel(ks_ref, vs_ref, sel_ref, out_ref, x_ref, buf, send_sem, recv_sem):
    s, r = lax.axis_index("seq"), lax.axis_index("inter")
    barrier = pltpu.get_barrier_semaphore()
    for k in range(1, NODES):
        pl.semaphore_signal(
            barrier, inc=1, device_id=(lax.rem(s + k, NODES), r), device_id_type=MESH
        )
    x_ref[...] = jnp.zeros_like(x_ref)
    x_ref[0:1, 0:ROWS_KV] = ks_ref[...].astype(jnp.float32)
    x_ref[0:1, ROWS_KV : 2 * ROWS_KV] = vs_ref[...].astype(jnp.float32)
    for j in range(2):
        x_ref[0:1, 64 + 3 * j : 67 + 3 * j] = sel_ref[j : j + 1].astype(jnp.float32)
    pl.semaphore_wait(barrier, NODES - 1)
    copies = []
    for k in range(1, NODES):
        copy = pltpu.make_async_remote_copy(
            src_ref=x_ref,
            dst_ref=buf.at[s],
            send_sem=send_sem.at[k],
            recv_sem=recv_sem.at[k],
            device_id=(lax.rem(s + k, NODES), r),
            device_id_type=MESH,
        )
        copy.start()
        copies.append(copy)
    buf[s] = x_ref[...]
    for copy in copies:
        copy.wait()
    out_ref[...] = buf[...]


def plan_kernel(
    rows, start, tab, send, place, limit, factor, flag, occ, bucket, cnt, tbl, posn, front
):
    me = lax.axis_index("seq")

    def clear(ref, count):
        def step(i, _):
            ref[i] = 0
            return 0

        lax.fori_loop(0, count, step, 0, unroll=8)

    clear(front, NODES * 8)
    for t in range(SLOTS):
        for d in range(4):
            tbl[(me * 4 + d) * 8 + t] = 0

    def sort_dest(dest, _):
        for jk in range(6):
            block = rows[dest, 0, 64 + jk].astype(jnp.int32)
            row = block >> 4
            pair = (block & (NODES - 1)) * NODES + dest
            steps = jnp.where(block * BLK < start[0], tab[DIST_AT + pair], 0)
            only = jnp.where(steps == 1, tab[pair * CANDS], NODES * 4)
            occ[only] = occ[only] + LOAD
            item = dest * 8 + jk
            posn[item] = row
            phase = jnp.where(front[item] > 0, 0, 1 + jk // 3)
            kind = jnp.where(steps == 0, 12, phase * 4 + 4 - steps)
            at = cnt[kind]
            bucket[kind * 96 + at] = (pair * CANDS) | (row << 16) | (item << 24)
            cnt[kind] = at + 1
        return 0

    def attempt(carry):
        clear(occ, NODES * 4)
        for kind in range(13):
            cnt[kind] = 0
        lax.fori_loop(0, NODES, sort_dest, 0)
        for kind in range(12):
            bucket[kind * 96 + cnt[kind]] = 0

        def run_phase(phase, missed):
            for hops in (4, 3, 2, 1):
                kind = phase * 4 + 4 - hops

                def fetch(i, kind=kind, hops=hops):
                    entry = bucket[kind * 96 + i]
                    return (entry,) + tuple(tab[(entry & 0xFFFF) + c] for c in range(CHOICES[hops]))

                def route(i, carry, hops=hops, fetch=fetch):
                    missed, entry = carry[:2]
                    upcoming = fetch(i + 1)
                    item = entry >> 24
                    row = (entry >> 16) & 255
                    best = None
                    for links in carry[2:]:
                        seen, words, ends = 0, 0, 0
                        for h in range(hops):
                            word = occ[(links >> (8 * h)) & 255]
                            used = word | seen
                            seen = used ^ (used + 1)
                            words = words + word
                            ends = ends + (seen << (8 * h))
                        cost = (seen << 16) + words
                        if best is None:
                            best, best_links, best_ends = cost, links, ends
                        else:
                            less = cost < best
                            best = jnp.where(less, cost, best)
                            best_links = jnp.where(less, links, best_links)
                            best_ends = jnp.where(less, ends, best_ends)
                    fits = best < jnp.where((item & 7) < 3, 1 << (16 + SLOTS_FIRST), 1 << (16 + SLOTS))
                    source = row
                    load = LOAD if hops > 1 else 0
                    for h in range(hops):
                        link = (best_links >> (8 * h)) & 255
                        end = (best_ends >> (8 * h)) & 255
                        occ[link] = occ[link] + jnp.where(fits, ((end + 1) >> 1) + load, 0)
                        slot = tab[SLOT_AT + end]
                        tbl[jnp.where(fits, link * 8 + slot, NODES * 4 * 8)] = source
                        source = ROWS_KV + 4 * slot + (link & 3)
                    posn[item] = jnp.where(fits, source, row)
                    late = jnp.where(fits, 0, 1)
                    front[item] = front[item] | late
                    return (missed + late,) + upcoming

                missed = lax.fori_loop(0, cnt[kind], route, (missed,) + fetch(0))[0]
            return missed

        return lax.fori_loop(0, 3, run_phase, jnp.int32(0)), carry[1] + 1

    missed, _ = lax.while_loop(
        lambda carry: (carry[0] > 0) & (carry[1] < TRIES), attempt, (jnp.int32(1), jnp.int32(0))
    )
    for t in range(SLOTS):
        for d in range(4):
            send[t * 4 + d] = tbl[(me * 4 + d) * 8 + t]
    for jk in range(6):
        block = rows[me, 0, 64 + jk].astype(jnp.int32)
        owner = block & (NODES - 1)
        row = block >> 4
        place[jk] = posn[me * 8 + jk]
        limit[jk] = start[0] - block * BLK
        factor[jk] = rows[owner, 0, row] * (LOG2E / math.sqrt(DH))
        factor[8 + jk] = rows[owner, 0, ROWS_KV + row]
    flag[...] = jnp.full((1, 128), missed, jnp.int32).astype(jnp.float32)


def main_kernel(
    send, place, limit, factor, flag, q, sk_hbm, sv_hbm, ck_hbm, cv_hbm,
    out, over,
    kp, vp, snd, rcv, qb, ob, sk, sv, acc, top, even, odd, even_top, odd_top, flags,
    load_sem, kv_send, kv_recv, q_send, q_recv, o_send, o_recv, f_send, f_recv,
):
    s, r = lax.axis_index("seq"), lax.axis_index("inter")
    z, x = s // SIDE, s % SIDE
    y, core = r // 2, r % 2
    beside = (
        z * SIDE + (x + 1) % SIDE,
        z * SIDE + (x + 3) % SIDE,
        (z + 1) % SIDE * SIDE + x,
        (z + 3) % SIDE * SIDE + x,
    )

    def peer(k):
        pair = k // 2
        dy = (2 + 3 * pair + 3 * (pair * (pair - 1) // 2)) % 4
        return (y + dy) % 4 * 2 + (core + 1 + k) % 2

    loads = [
        pltpu.make_async_copy(ck_hbm.at[:, 0], kp.at[pl.ds(0, ROWS_KV)], load_sem.at[0]),
        pltpu.make_async_copy(cv_hbm.at[:, 0], vp.at[pl.ds(0, ROWS_KV)], load_sem.at[1]),
        pltpu.make_async_copy(sk_hbm.at[:, 0], sk, load_sem.at[2]),
        pltpu.make_async_copy(sv_hbm.at[:, 0], sv, load_sem.at[3]),
        pltpu.make_async_copy(
            q.at[:, 0, :, pl.ds(pl.multiple_of(r * WIDE, WIDE), WIDE)],
            qb.at[:, pl.ds(pl.multiple_of(r * QROWS, QROWS), QROWS)],
            load_sem.at[4],
        ),
    ]
    for load in loads:
        load.start()

    barrier = pltpu.get_barrier_semaphore()
    for n in beside:
        pl.semaphore_signal(barrier, inc=1, device_id=(n, r), device_id_type=MESH)
    for k in range(PEERS - 1):
        pl.semaphore_signal(barrier, inc=1, device_id=(s, peer(k)), device_id_type=MESH)
    pl.semaphore_wait(barrier, PEERS + 3)

    def kv_copy(t, d, h):
        return pltpu.make_async_remote_copy(
            src_ref=snd.at[t, d, h],
            dst_ref=rcv.at[t, d, h],
            send_sem=kv_send.at[t, d, h],
            recv_sem=kv_recv.at[t, d, h],
            device_id=(beside[d], r),
            device_id_type=MESH,
        )

    def q_copy(k):
        to = peer(k)
        return pltpu.make_async_remote_copy(
            src_ref=q.at[:, 0, :, pl.ds(pl.multiple_of(to * WIDE, WIDE), WIDE)],
            dst_ref=qb.at[:, pl.ds(pl.multiple_of(r * QROWS, QROWS), QROWS)],
            send_sem=q_send.at[k],
            recv_sem=q_recv.at[k],
            device_id=(s, to),
            device_id_type=MESH,
        )

    def f_copy(k):
        return pltpu.make_async_remote_copy(
            src_ref=flag,
            dst_ref=flags.at[r],
            send_sem=f_send.at[k],
            recv_sem=f_recv.at[k],
            device_id=(s, peer(k)),
            device_id_type=MESH,
        )

    def o_copy(j, k):
        to = peer(k)
        return pltpu.make_async_remote_copy(
            src_ref=ob.at[j, pl.ds(pl.multiple_of(to * QROWS, QROWS), QROWS)],
            dst_ref=out.at[j, 0, :, pl.ds(pl.multiple_of(r * WIDE, WIDE), WIDE)],
            send_sem=o_send.at[j, k],
            recv_sem=o_recv.at[j, k],
            device_id=(s, to),
            device_id_type=MESH,
        )

    def o_own(j):
        return pltpu.make_async_copy(
            ob.at[j, pl.ds(pl.multiple_of(r * QROWS, QROWS), QROWS)],
            out.at[j, 0, :, pl.ds(pl.multiple_of(r * WIDE, WIDE), WIDE)],
            load_sem.at[5 + j],
        )

    def pump(t, h):
        pool = (kp, vp)[h]
        if t > 0:
            for d in range(4):
                kv_copy(t - 1, d, h).wait_recv()
            for d in range(4):
                pool[ROWS_KV + 4 * (t - 1) + d] = rcv[t - 1, d, h]
        if t < SLOTS:
            for d in range(4):
                snd[t, d, h] = pool[send[t * 4 + d]]
                kv_copy(t, d, h).start()

    def rows_of(c):
        return pl.ds(pl.multiple_of(c * QROWS, QROWS), QROWS)

    def load_q(j, c):
        tile = qb[j, rows_of(c), :]
        return jnp.concatenate([tile[:, h * DH : (h + 1) * DH] for h in range(HG)], axis=0)

    def scores_of(query, keys):
        return lax.dot_general(
            query, keys, (((1,), (1,)), ((), ())), preferred_element_type=jnp.float32
        )

    ones = jnp.ones((BLK, DH), jnp.bfloat16)
    column = lax.broadcasted_iota(jnp.int32, (1, BLK), 1)

    def own_tile(j, c):
        scores = scores_of(load_q(j, c), sk[j]) * (LOG2E / math.sqrt(DH))
        row = lax.broadcasted_iota(jnp.int32, (TILE_ROWS, 1), 0) % QROWS + c * QROWS
        scores = jnp.where(column <= row, scores, NEG)
        high = jnp.max(scores, axis=1, keepdims=True)
        weights = jnp.exp2(scores - high).astype(jnp.bfloat16)
        acc[j, c] = jnp.dot(
            weights, jnp.concatenate([sv[j], ones], axis=1), preferred_element_type=jnp.float32
        )
        top[j, c] = jnp.broadcast_to(high, (TILE_ROWS, DH))

    def score(j, k, held, held_top):
        c = peer(k)
        query = load_q(j, c)
        high = top[j, c][:, :1]
        for i in range(3):
            bias = jnp.where(column < limit[3 * j + i], 0.0, NEG)
            part = scores_of(query, kp[place[3 * j + i]]) * factor[3 * j + i] + bias
            high = jnp.maximum(high, jnp.max(part, axis=1, keepdims=True))
            held[i] = part
        held_top[...] = jnp.broadcast_to(high, (TILE_ROWS, DH))

    def attend_tile(j, k, held, held_top):
        c = peer(k)
        high = held_top[...]
        fade = jnp.exp2(top[j, c] - high)
        old = acc[j, c]
        summed = old[:, :DH] * fade
        total = old[:, DH:] * fade
        for i in range(3):
            weights = jnp.exp2(held[i] - high[:, :1]).astype(jnp.bfloat16)
            more = jnp.dot(
                weights,
                jnp.concatenate([vp[place[3 * j + i]], ones], axis=1),
                preferred_element_type=jnp.float32,
            )
            summed = summed + more[:, :DH] * factor[8 + 3 * j + i]
            total = total + more[:, DH:]
        done = (summed / total).astype(jnp.bfloat16)
        for h in range(HG):
            ob[j, rows_of(c), h * DH : (h + 1) * DH] = done[h * QROWS : (h + 1) * QROWS]

    def own_block(j, begin, end):
        def step(c, _):
            own_tile(j, c)
            return 0

        lax.fori_loop(begin, end, step, 0)

    def cache_blocks(j, begin, end):
        def step(pair, _):
            score(j, 2 * pair + 1, odd, odd_top)
            attend_tile(j, 2 * pair, even, even_top)
            o_copy(j, 2 * pair).start()
            score(j, 2 * pair + 2, even, even_top)
            attend_tile(j, 2 * pair + 1, odd, odd_top)
            o_copy(j, 2 * pair + 1).start()
            return 0

        if begin == 0:
            score(j, 0, even, even_top)
        lax.fori_loop(begin // 2, min(end, PEERS - 2) // 2, step, 0)
        if end == PEERS:
            score(j, PEERS - 1, odd, odd_top)
            attend_tile(j, PEERS - 2, even, even_top)
            o_copy(j, PEERS - 2).start()
            attend_tile(j, PEERS - 1, odd, odd_top)
            o_own(j).start()

    for k in range(PEERS - 1):
        q_copy(k).start()
    loads[0].wait()
    pump(0, 0)
    loads[1].wait()
    pump(0, 1)
    for k in range(PEERS - 1):
        f_copy(k).start()
    flags[r] = flag[...]
    for load in loads[2:]:
        load.wait()
    for t in range(1, SLOTS + 1):
        for h in range(2):
            pump(t, h)
            if (t, h) == (3, 0):
                for k in range(PEERS - 1):
                    q_copy(k).wait()
                own_block(0, 0, 4)
            if (t, h) == (3, 1):
                own_block(0, 4, PEERS)
            if (t, h) == (4, 0):
                own_block(1, 0, 4)
            if (t, h) == (SLOTS - 1, 1):
                own_block(1, 4, PEERS)
            if (t, h) == (SLOTS_FIRST, 1):
                cache_blocks(0, 0, 2)
            if (t, h) == (SLOTS_FIRST + 1, 0):
                cache_blocks(0, 2, 4)
            if (t, h) == (SLOTS_FIRST + 1, 1):
                cache_blocks(0, 4, PEERS)
    cache_blocks(1, 0, PEERS)
    for k in range(PEERS - 1):
        f_copy(k).wait()
    worst = flags[0]
    for k in range(1, PEERS):
        worst = jnp.maximum(worst, flags[k])
    over[...] = worst
    for t in range(SLOTS):
        for d in range(4):
            for h in range(2):
                kv_copy(t, d, h).wait_send()
    for j in range(2):
        o_own(j).wait()
        for k in range(PEERS - 1):
            o_copy(j, k).wait()


def copy_kernel(x, out, sem):
    copies = [pltpu.make_async_copy(x.at[j], out.at[j], sem.at[j]) for j in range(2)]
    for copy in copies:
        copy.start()
    for copy in copies:
        copy.wait()


def settle(attended):
    hbm = pl.BlockSpec(memory_space=pl.ANY)
    return pl.pallas_call(
        copy_kernel,
        out_shape=jax.ShapeDtypeStruct(attended.shape, attended.dtype),
        in_specs=[hbm],
        out_specs=hbm,
        scratch_shapes=[pltpu.SemaphoreType.DMA((2,))],
        name="settle",
    )(attended)


def per_device(
    queries, span_keys, span_values, cache_keys, cache_values, key_scales, value_scales, selections, start
):
    f32, i32, bf16 = jnp.float32, jnp.int32, jnp.bfloat16
    smem = pl.BlockSpec(memory_space=pltpu.SMEM)
    vmem = pl.BlockSpec(memory_space=pltpu.VMEM)
    hbm = pl.BlockSpec(memory_space=pl.ANY)
    dma = pltpu.SemaphoreType.DMA
    rows = pl.pallas_call(
        lists_kernel,
        out_shape=jax.ShapeDtypeStruct((NODES, 1, 128), f32),
        in_specs=[vmem] * 3,
        out_specs=vmem,
        scratch_shapes=[
            pltpu.VMEM((1, 128), f32),
            pltpu.VMEM((NODES, 1, 128), f32),
            dma((NODES,)),
            dma((NODES,)),
        ],
        compiler_params=pltpu.CompilerParams(collective_id=0, has_side_effects=True),
        name="lists",
    )(key_scales.reshape(1, ROWS_KV), value_scales.reshape(1, ROWS_KV), selections.reshape(2, 3))
    send, place, limit, factor, flag = pl.pallas_call(
        plan_kernel,
        out_shape=(
            jax.ShapeDtypeStruct((4 * SLOTS,), i32),
            jax.ShapeDtypeStruct((8,), i32),
            jax.ShapeDtypeStruct((8,), i32),
            jax.ShapeDtypeStruct((16,), f32),
            jax.ShapeDtypeStruct((1, 128), f32),
        ),
        in_specs=[smem] * 3,
        out_specs=(smem, smem, smem, smem, vmem),
        scratch_shapes=[
            pltpu.SMEM((NODES * 4 + 8,), i32),
            pltpu.SMEM((13 * 96 + 8,), i32),
            pltpu.SMEM((16,), i32),
            pltpu.SMEM((NODES * 4 * 8 + 8,), i32),
            pltpu.SMEM((NODES * 8,), i32),
            pltpu.SMEM((NODES * 8,), i32),
        ],
        name="plan",
    )(rows, start, jnp.asarray(TABLES))
    attended, over = pl.pallas_call(
        main_kernel,
        out_shape=(
            jax.ShapeDtypeStruct(queries.shape, bf16),
            jax.ShapeDtypeStruct((1, 128), f32),
        ),
        in_specs=[smem] * 4 + [vmem] + [hbm] * 5,
        out_specs=(hbm, vmem),
        scratch_shapes=[
            pltpu.VMEM((POOL, BLK, DH), bf16),
            pltpu.VMEM((POOL, BLK, DH), bf16),
            pltpu.VMEM((SLOTS, 4, 2, BLK, DH), bf16),
            pltpu.VMEM((SLOTS, 4, 2, BLK, DH), bf16),
            pltpu.VMEM((2, BLK, WIDE), bf16),
            pltpu.VMEM((2, BLK, WIDE), bf16),
            pltpu.VMEM((2, BLK, DH), bf16),
            pltpu.VMEM((2, BLK, DH), bf16),
            pltpu.VMEM((2, PEERS, TILE_ROWS, 2 * DH), f32),
            pltpu.VMEM((2, PEERS, TILE_ROWS, DH), f32),
            pltpu.VMEM((3, TILE_ROWS, BLK), f32),
            pltpu.VMEM((3, TILE_ROWS, BLK), f32),
            pltpu.VMEM((TILE_ROWS, DH), f32),
            pltpu.VMEM((TILE_ROWS, DH), f32),
            pltpu.VMEM((PEERS, 1, 128), f32),
            dma((8,)),
            dma((SLOTS, 4, 2)),
            dma((SLOTS, 4, 2)),
            dma((PEERS,)),
            dma((PEERS,)),
            dma((2, PEERS)),
            dma((2, PEERS)),
            dma((PEERS,)),
            dma((PEERS,)),
        ],
        compiler_params=pltpu.CompilerParams(
            collective_id=1, has_side_effects=True, vmem_limit_bytes=56 * 2**20
        ),
        name="exchange_attend",
    )(send, place, limit, factor, flag, queries, span_keys, span_values, cache_keys, cache_values)
    return lax.cond(
        over[0, 0] > 0,
        lambda: padded(queries, span_keys, span_values, cache_keys, cache_values, start, rows),
        lambda: settle(attended),
    )


def solution(mesh):
    placed = (
        P(None, "seq", "inter", None),
        P(None, "seq", None, "inter"),
        P(None, "seq", None, "inter"),
        P(None, "seq", None, "inter"),
        P(None, "seq", None, "inter"),
        P(None, "seq", "inter"),
        P(None, "seq", "inter"),
        P(None, "seq", "inter", None),
        P(),
    )
    return jax.shard_map(
        per_device,
        mesh=mesh,
        in_specs=placed,
        out_specs=P(None, "seq", "inter", None),
        check_vma=False,
    )
```
